32 devices in a mesh: group: 2 (over y), frame: 4 (over z), head: 2 (over x), sub: 2 (over core).
Axes of the slice: x: 2, y: 2, z: 4, core: 2. Of those that a mesh axis runs over, the one named last changes fastest.
Arguments:
- queries: bfloat16 [6144, 2560], P(('group', 'frame', 'sub'), 'head'), parts along dimension 0, may hold values from -12 to 12
- keys: bfloat16 [6144, 2560], P(('group', 'frame', 'sub'), 'head'), parts along dimension 0, may hold values from -4 to 4
- values: bfloat16 [6144, 2560], P(('group', 'frame', 'sub'), 'head'), parts along dimension 0, may hold values from -6 to 6
- out_weight: bfloat16 [2560, 5120], P(('frame', 'sub'), 'head'), may hold values from -0.125 to 0.125
- time_table: bfloat16 [50, 5120], P(None, 'head'), may hold values from -4 to 4
- action_table: bfloat16 [256, 5120], P(None, 'head'), may hold values from -4 to 4
- levels: int32 [8], P('group'), parts along dimension 0, may hold values from 0 to 49
- actions: int32 [8, 4], P('group'), parts along dimension 0, may hold values from 0 to 255
- cycle_order: int32 [8], P('group'), parts along dimension 0, may hold values from 0 to 3, as said below
Outputs:
- velocity: bfloat16 [6144, 5120], P(('group', 'frame', 'sub'), 'head'), parts along dimension 0
The draws below stay inside these ranges and needn't reach their ends.
There are 2 independent parts, one for each index of `group`. The reference program is written for one: setup_inputs(seed, part) draws one part's arguments, and reference() takes and returns one part's arrays. A program takes and returns all parts, laid end to end along the dimension named above; an argument that names none is the same for every part. Nothing has to cross between parts.
Inputs may be any that keep to these rules, and one draw needn't show every extreme that they name: cycle_order[s] = (s + R) mod 4 for one R of the draw; each position appears once.
All inputs are finite; a program needn't handle non-finite values.
Results may differ from the reference program's by a relative error of at most 0.0056.
Values may be sent and summed in bfloat16 or wider, within the bound.
A program may use at most 64 MiB of HBM per device.

```python
import jax
import jax.numpy as jnp
from jax import lax

D = 5120
HEAD_DIM = 128
LEVELS = 50
ACTIONS = 256
APF = 4
FWIN = 3
HW = 2560
TOKF = 768
FRAMES = 4
TOKENS = 3072


def drawn_pair(key):
    base_query = jax.random.normal(jax.random.fold_in(key, 101), (TOKENS, HW), jnp.float32)
    base_key = jax.random.normal(jax.random.fold_in(key, 102), (TOKENS, HW), jnp.float32)
    return (base_query, base_key)


def draw_queries(key, part):
    base_query, base_key = drawn_pair(key)
    drawn = jnp.clip(base_query, -4.0, 4.0)
    return drawn.astype(jnp.bfloat16)


def draw_keys(key, part):
    base_query, base_key = drawn_pair(key)
    drawn = jnp.clip(base_key, -4.0, 4.0)
    return drawn.astype(jnp.bfloat16)


def draw_cycle_order(key, part):
    key = jax.random.fold_in(key, 7)
    offset = jax.random.randint(key, (), 0, FRAMES)
    return ((jnp.arange(FRAMES, dtype=jnp.int32) + offset) % FRAMES).astype(jnp.int32)


def touch_ends(values, key, low, top_value):
    extent = values.shape
    index_at = [jax.random.randint(jax.random.fold_in(key, axis), (), 0, extent[axis]) for axis in range(len(extent))]
    values = values.at[tuple(index_at)].set(low)
    longest = extent.index(max(extent))
    index_at[longest] = (index_at[longest] + 1) % extent[longest]
    return values.at[tuple(index_at)].set(top_value)


def block_scale(stream_key, dims, split, low, top_value):
    factor_of, own = 1.0, jax.random.fold_in(stream_key, 6)
    for dim, blocks in split:
        steps = jnp.exp(jax.random.uniform(jax.random.fold_in(own, dim), (blocks,), jnp.float32, low / len(split), top_value / len(split)))
        factor_of = factor_of * jnp.repeat(steps, dims[dim] // blocks).reshape([-1 if axis == dim else 1 for axis in range(len(dims))])
    return factor_of


def bell_draw(rng, dims, scale, reach, split=(), held_as=jnp.bfloat16):
    level = block_scale(rng, dims, split, -0.22, 0.18) if split else 1.0
    values = jax.random.normal(rng, dims, jnp.float32) * scale * level
    return jnp.minimum(jnp.maximum(values, -reach), reach).astype(held_as)


def setup_inputs(seed: int = 0, part: int = 0) -> dict:
    streams_of = jax.random.split(jax.random.key(seed), 10)
    part_splits = jax.random.split(jax.random.fold_in(streams_of[9], part), 10)
    queries = draw_queries(jax.random.fold_in(jax.random.fold_in(streams_of[9], part), 71), part)
    keys = draw_keys(jax.random.fold_in(jax.random.fold_in(streams_of[9], part), 71), part)
    values = bell_draw(part_splits[2], (TOKENS, HW), 1.0, 6.0, ((0, 8), (1, 2)))
    out_weight = bell_draw(streams_of[3], (HW, D), HW ** -0.5, 0.125, ((0, 8), (1, 2)))
    time_table = bell_draw(streams_of[4], (LEVELS, D), 0.6, 4.0, ((1, 2),))
    action_table = bell_draw(streams_of[5], (ACTIONS, D), 0.4, 4.0, ((1, 2),))
    levels = touch_ends(jax.random.randint(part_splits[6], (FRAMES,), 0, LEVELS), jax.random.fold_in(part_splits[6], 1), 0, LEVELS - 1).astype(jnp.int32)
    actions = touch_ends(jax.random.randint(part_splits[7], (FRAMES, APF), 0, ACTIONS), jax.random.fold_in(part_splits[7], 1), 0, ACTIONS - 1).astype(jnp.int32)
    cycle_order = draw_cycle_order(jax.random.fold_in(jax.random.fold_in(streams_of[9], part), 71), part)
    return dict(queries=queries, keys=keys, values=values, out_weight=out_weight, time_table=time_table, action_table=action_table, levels=levels, actions=actions, cycle_order=cycle_order)


def attend_frame(query_rows, key_rows, value_rows, key_valid):
    query_count = query_rows.shape[0]
    length = key_rows.shape[0]
    row_width = query_rows.shape[1]
    head_count = row_width // HEAD_DIM
    query_heads = jnp.moveaxis(query_rows.reshape(query_count, head_count, HEAD_DIM), 1, 0)
    key_heads = jnp.moveaxis(key_rows.reshape(length, head_count, HEAD_DIM), 1, 0)
    value_heads = jnp.moveaxis(value_rows.reshape(length, head_count, HEAD_DIM), 1, 0)
    factor = HEAD_DIM ** -0.5

    def one_head(operands):
        query_one, key_one, value_one = operands
        scores = jnp.dot(query_one, key_one.T, preferred_element_type=jnp.float32) * factor
        scores = jnp.where(key_valid[None, :], scores, -1e30)
        largest = jnp.max(scores, axis=1, keepdims=True)
        weights = jnp.exp(scores - largest)
        totals = jnp.sum(weights, axis=1, keepdims=True)
        mixed_rows = jnp.dot(weights.astype(jnp.bfloat16), value_one, preferred_element_type=jnp.float32)
        return (mixed_rows / totals).astype(jnp.bfloat16)

    result = lax.map(one_head, (query_heads, key_heads, value_heads))
    return jnp.moveaxis(result, 0, 1).reshape(query_count, row_width)


def reference(queries, keys, values, out_weight, time_table, action_table, levels, actions, cycle_order):
    query_frames = queries.reshape(FRAMES, TOKF, HW)
    key_frames = keys.reshape(FRAMES, TOKF, HW)
    value_frames = values.reshape(FRAMES, TOKF, HW)
    offsets = jnp.arange(FWIN, dtype=jnp.int32)

    def one_frame(frame_slot):
        near_slots = ((frame_slot - offsets) % FRAMES).astype(jnp.int32)
        block_valid = cycle_order[near_slots] == cycle_order[frame_slot] - offsets
        key_valid = jnp.repeat(block_valid, TOKF)
        key_rows = key_frames[near_slots].reshape(FWIN * TOKF, HW)
        value_rows = value_frames[near_slots].reshape(FWIN * TOKF, HW)
        return attend_frame(query_frames[frame_slot], key_rows, value_rows, key_valid)

    attended = lax.map(one_frame, jnp.arange(FRAMES, dtype=jnp.int32)).reshape(TOKENS, HW)
    projected = jnp.dot(attended, out_weight, preferred_element_type=jnp.float32)
    gate_rows = time_table[levels].astype(jnp.float32) + jnp.sum(action_table[actions].astype(jnp.float32), axis=1)
    velocity = projected.reshape(FRAMES, TOKF, D) * gate_rows[:, None, :]
    return velocity.reshape(TOKENS, D).astype(jnp.bfloat16)
```

```python
import functools

import jax
import jax.numpy as jnp
from jax import lax
from jax.experimental import pallas as pl
from jax.experimental.pallas import tpu as pltpu
from jax.sharding import PartitionSpec as P

HEAD_DIM = 128
LEVELS = 50
ACTIONS = 256
FWIN = 3
PIECES = 5
LOG2E = 1.4426950408889634
MESH = pl.DeviceIdType.MESH


def from_behind(array, axis, by):
    count = lax.axis_size(axis)
    return lax.ppermute(array, axis, [(i, (i + by) % count) for i in range(count)])


def attend_heads(query_rows, key_rows, value_rows, key_valid):
    query_count = query_rows.shape[0]
    length = key_rows.shape[0]
    row_width = query_rows.shape[1]
    head_count = row_width // HEAD_DIM
    query_heads = jnp.moveaxis(query_rows.reshape(query_count, head_count, HEAD_DIM), 1, 0)
    key_heads = jnp.moveaxis(key_rows.reshape(length, head_count, HEAD_DIM), 1, 0)
    value_heads = jnp.moveaxis(value_rows.reshape(length, head_count, HEAD_DIM), 1, 0)
    factor = HEAD_DIM ** (-0.5)

    def one_head(operands):
        query_one, key_one, value_one = operands
        scores = jnp.dot(query_one, key_one.T, preferred_element_type=jnp.float32) * factor
        scores = jnp.where(key_valid[None, :], scores, -1e30)
        largest = jnp.max(scores, axis=1, keepdims=True)
        weights = jnp.exp(scores - largest)
        totals = jnp.sum(weights, axis=1, keepdims=True)
        mixed_rows = jnp.dot(
            weights.astype(jnp.bfloat16), value_one, preferred_element_type=jnp.float32
        )
        return (mixed_rows / totals).astype(jnp.bfloat16)

    result = lax.map(one_head, (query_heads, key_heads, value_heads))
    return jnp.moveaxis(result, 0, 1).reshape(query_count, row_width)


def gate_of_slot(time_table, action_table, levels, actions):
    frame_slot = lax.axis_index("frame")
    level_onehot = (jnp.arange(LEVELS, dtype=jnp.int32) == levels[frame_slot]).astype(jnp.bfloat16)
    action_match = jnp.arange(ACTIONS, dtype=jnp.int32)[None, :] == actions[frame_slot][:, None]
    action_count = jnp.sum(action_match.astype(jnp.float32), axis=0).astype(jnp.bfloat16)
    gate_row = jnp.dot(level_onehot[None, :], time_table, preferred_element_type=jnp.float32)
    return gate_row + jnp.dot(
        action_count[None, :], action_table, preferred_element_type=jnp.float32
    )


def ring_shards(
    queries, keys, values, out_weight, time_table, action_table, levels, actions, cycle_order
):
    window = FWIN
    own_position = cycle_order[lax.axis_index("frame")]
    gate_row = gate_of_slot(time_table, action_table, levels, actions)
    paired = jnp.stack([keys, values])
    block_rows = paired.shape[1] * lax.axis_size("sub")
    local_pair = lax.all_gather(paired, "sub", axis=1, tiled=True)
    blocks = [local_pair]
    for distance in range(1, window):
        blocks.append(from_behind(local_pair, "frame", distance))
    joined = jnp.concatenate(blocks, axis=1)
    block_valid = own_position >= jnp.arange(window, dtype=jnp.int32)
    key_valid = jnp.repeat(block_valid, block_rows)
    attended = attend_heads(queries, joined[0], joined[1], key_valid)
    outputs = lax.all_gather(attended, "head", axis=1, tiled=True)
    all_rows = lax.all_gather(out_weight, ("frame", "sub"), axis=0, tiled=True)
    projected = jnp.dot(outputs, all_rows, preferred_element_type=jnp.float32)
    return (gate_row * projected).astype(jnp.bfloat16)


class Indices:
    def __init__(self, sems):
        self.sems, self.names, self.used = sems, {}, 0

    def __call__(self, name, count=1):
        if name not in self.names:
            self.names[name] = (self.used, count)
            self.used += count
        return self.names[name][0]


def line_kernel(
    cycle, q, k, v, w, gate, out,
    kb, vb, qb, stat, acc, attf, aout, wf, pacc, send_sems, recv_sems, local_sems,
):
    rows, cols = q.shape
    wrows, wide = w.shape
    half = wrows // 2
    part = half // PIECES
    heads = cols // HEAD_DIM
    per = heads // PIECES
    att_cols = per * HEAD_DIM
    keys_n = 2 * rows
    scale = HEAD_DIM ** (-0.5) * LOG2E

    g, f, h, c = (lax.axis_index(name) for name in ("group", "frame", "head", "sub"))
    side = f // 2
    f_in, f_out = 1 + side, 3 * side
    peer_in, peer_out = 2 - side, 3 - 3 * side
    inner = f == f_in
    mate = f_in + f_out - f
    sub_dev = (g, f, h, 1 - c)
    x_dev = (g, f, 1 - h, c)
    y_dev = (1 - g, f, h, c)
    mate_dev = (g, mate, h, c)
    peer_dev = (g, peer_in, h, c)

    barrier = pltpu.get_barrier_semaphore()
    for dev in (sub_dev, x_dev, y_dev, mate_dev):
        pl.semaphore_signal(barrier, inc=1, device_id=dev, device_id_type=MESH)

    @pl.when(inner)
    def _():
        pl.semaphore_signal(barrier, inc=1, device_id=peer_dev, device_id_type=MESH)
        pl.semaphore_wait(barrier, 5)

    @pl.when(jnp.logical_not(inner))
    def _():
        pl.semaphore_wait(barrier, 4)

    sends, recvs = Indices(send_sems), Indices(recv_sems)

    def copy(src, dst, send, recv, dev):
        return pltpu.make_async_remote_copy(
            src_ref=src,
            dst_ref=dst,
            send_sem=send_sems.at[send],
            recv_sem=recv_sems.at[recv],
            device_id=dev,
            device_id_type=MESH,
        )

    def arrived(dst, recv):
        copy(dst, dst, 0, recv, sub_dev).wait_recv()

    def own_rows(base, count, index):
        return pl.ds(pl.multiple_of(base + index * count, 16), count)

    def kv_half(buf, block, cc):
        return buf.at[block, own_rows(0, rows, cc), :]

    def w_shard(block, cc):
        return wf.at[block, own_rows(0, wrows, cc), :]

    def w_piece(block, cc, gg):
        return wf.at[block, own_rows(cc * wrows, half, gg), :]

    def w_part(block, cc, gg, i):
        return wf.at[block, own_rows(cc * wrows + gg * half, part, i), :]

    def att_part(ref, i):
        return ref.at[:, pl.ds(pl.multiple_of(i * att_cols, HEAD_DIM), att_cols)]

    kv_z = lambda n, which: recvs("kvz" + n + which)
    kv_s = lambda n, which: recvs("kvs" + n + which)
    wz = {b: recvs("wz" + b, PIECES) for b in ("mate", "pi", "po")}
    wy = {b: recvs("wy" + b, PIECES) for b in ("mate", "pi", "po")}
    ws = {b: recvs("ws" + b, 2) for b in ("mate", "pi", "po")}
    ws_own, rq = recvs("wsown"), recvs("q")
    ra, rx = recvs("ra", PIECES), recvs("rx", PIECES)
    wblock = {"mate": mate, "pi": peer_in, "po": peer_out}

    def w_to_sub(b, gg, which):
        src = w_piece(wblock[b], c, gg)
        one = copy(src, src, sends("wsub" + b + str(which)), ws[b] + which, sub_dev)
        one.start()

    def w_piece_to_y(b):
        src = w_piece(wblock[b], c, g)
        copy(src, src, sends("wyp" + b, PIECES), wy[b], y_dev).start()

    def w_part_to_y(b, i):
        src = w_part(wblock[b], c, g, i)
        copy(src, src, sends("wyp" + b, PIECES) + i, wy[b] + i, y_dev).start()

    def w_part_to_mate(b, i):
        src = w_part(wblock[b], c, g, i)
        copy(src, src, sends("wout" + b, PIECES) + i, wz[b] + i, mate_dev).start()

    def valid_of(slot, block):
        distance = (slot - block + 4) % 4
        return cycle[block] == cycle[slot] - distance

    def unit(si, block, head, finish=None):
        slot = jnp.where(si == 0, f_in, f_out)
        valid = valid_of(slot, block)
        lanes = pl.ds(pl.multiple_of(head * HEAD_DIM, HEAD_DIM), HEAD_DIM)
        si_head = si * heads + head
        scores = lax.dot_general(
            qb[si, :, lanes], kb[block, :, lanes], (((1,), (1,)), ((), ())),
            preferred_element_type=jnp.float32,
        )
        old = stat[si_head]
        old_max, old_total = old[:, :1], old[:, 64:65]
        block_max = jnp.where(valid, jnp.max(scores, axis=1, keepdims=True), -1e30)
        new_max = jnp.maximum(old_max, block_max)
        weights = jnp.exp2((scores - jnp.where(valid, new_max, 1e30)) * scale)
        fade = jnp.exp2((old_max - new_max) * scale)
        total = old_total * fade + jnp.sum(weights, axis=1, keepdims=True)
        mixed = acc[si_head] * fade + jnp.dot(
            weights.astype(jnp.bfloat16), vb[block, :, lanes], preferred_element_type=jnp.float32
        )
        if finish is None:
            acc[si_head] = mixed
            lane = lax.broadcasted_iota(jnp.int32, (rows, HEAD_DIM), 1)
            stat[si_head] = jnp.where(lane < 64, new_max, total)
        else:
            finish[:, lanes] = (mixed / total).astype(jnp.bfloat16)

    def units(si, block):
        @pl.loop(0, heads)
        def _(head):
            unit(si, block, head)

    def each_part(body):
        @pl.loop(0, PIECES)
        def _(i):
            body(i)

    own_w = pltpu.make_async_copy(w, w_shard(f, c), local_sems.at[0])
    own_w.start()
    w_to_partner = copy(w, w_shard(f, c), sends("wown"), ws_own, sub_dev)

    @pl.when(inner)
    def _():
        for n, ref, buf in (("k", k, kb), ("v", v, vb)):
            copy(ref, kv_half(buf, f, c), sends("i_sub" + n), kv_s(n, "i"), sub_dev).start()
            copy(ref, kv_half(buf, f, c), sends("i_peer" + n), kv_z(n, "pi"), peer_dev).start()
        locals_ = [
            pltpu.make_async_copy(k, kv_half(kb, f, c), local_sems.at[1]),
            pltpu.make_async_copy(v, kv_half(vb, f, c), local_sems.at[2]),
            pltpu.make_async_copy(q, qb.at[0], local_sems.at[3]),
        ]
        for one in locals_:
            one.start()
        w_to_partner.start()
        copy(
            w.at[own_rows(0, half, g), :], w_piece(f, c, g), sends("w_in_out"), wz["mate"], mate_dev
        ).start()

        @pl.loop(0, 2 * heads)
        def _(i):
            acc[i] = jnp.zeros((rows, HEAD_DIM), jnp.float32)
            lane = lax.broadcasted_iota(jnp.int32, (rows, HEAD_DIM), 1)
            stat[i] = jnp.where(lane < 64, -1e30, 0.0)

        for one in locals_:
            one.wait()
        for n, buf in (("k", kb), ("v", vb)):
            arrived(kv_half(buf, f, 1 - c), kv_s(n, "i"))
        units(0, f_in)
        for n, buf in (("k", kb), ("v", vb)):
            src = kv_half(buf, f_out, c)
            arrived(src, kv_z(n, "o"))
            copy(src, src, sends("o_peer" + n), kv_z(n, "po"), peer_dev).start()
            copy(src, src, sends("o_sub" + n), kv_s(n, "o"), sub_dev).start()
        for n, buf in (("k", kb), ("v", vb)):
            src = kv_half(buf, peer_in, c)
            arrived(src, kv_z(n, "pi"))
            copy(src, src, sends("pi_sub" + n), kv_s(n, "pi"), sub_dev).start()
        for n, buf in (("k", kb), ("v", vb)):
            arrived(kv_half(buf, f_out, 1 - c), kv_s(n, "o"))
            arrived(kv_half(buf, peer_in, 1 - c), kv_s(n, "pi"))
        units(0, jnp.where(side == 0, f_out, peer_in))
        arrived(qb.at[1], rq)
        units(1, f_out)
        units(1, peer_in)
        arrived(w_piece(mate, c, g), wz["mate"])
        w_piece_to_y("mate")
        w_to_sub("mate", g, 0)
        for n, buf in (("k", kb), ("v", vb)):
            src = kv_half(buf, peer_out, c)
            arrived(src, kv_z(n, "po"))
            copy(src, src, sends("po_sub" + n), kv_s(n, "po"), sub_dev).start()
        own_w.wait()

        def w_to_peer(i):
            src = w_part(f, c, g, i)
            copy(src, src, sends("w_own_peer", PIECES) + i, wz["pi"] + i, peer_dev).start()

        def mate_w_to_peer(i):
            src = w_part(mate, c, g, i)
            copy(src, src, sends("w_mate_peer", PIECES) + i, wz["po"] + i, peer_dev).start()

        each_part(w_to_peer)
        each_part(mate_w_to_peer)
        for n, buf in (("k", kb), ("v", vb)):
            arrived(kv_half(buf, peer_out, 1 - c), kv_s(n, "po"))
        last_block = jnp.where(side == 0, peer_out, f_in)

        def last(i):
            @pl.loop(0, per)
            def _(j):
                unit(1, last_block, i * per + j, aout)
                unit(0, peer_out, i * per + j, attf.at[h])

            src = att_part(aout, i)
            copy(src, att_part(attf.at[h], i), sends("aout", PIECES) + i, ra + i, mate_dev).start()
            src = att_part(attf.at[h], i)
            copy(src, src, sends("ax", PIECES) + i, rx + i, x_dev).start()
            arrived(w_part(peer_in, c, g, i), wz["pi"] + i)
            w_part_to_mate("pi", i)
            w_part_to_y("pi", i)

        each_part(last)
        arrived(w_piece(mate, c, 1 - g), wy["mate"])
        w_to_sub("mate", 1 - g, 1)
        w_to_sub("pi", g, 0)

        def po(i):
            arrived(w_part(peer_out, c, g, i), wz["po"] + i)
            w_part_to_mate("po", i)
            w_part_to_y("po", i)

        each_part(po)

    @pl.when(jnp.logical_not(inner))
    def _():
        first = [
            copy(k, kv_half(kb, f, c), sends("out_k"), kv_z("k", "o"), mate_dev),
            copy(v, kv_half(vb, f, c), sends("out_v"), kv_z("v", "o"), mate_dev),
        ]
        for one in first:
            one.start()
        w_to_partner.start()
        own_w.wait()
        arrived(w_piece(mate, c, g), wz["mate"])
        w_piece_to_y("mate")
        w_to_sub("mate", g, 0)
        for one in first:
            one.wait_send()
        q_copy = copy(q, qb.at[1], sends("out_q"), rq, mate_dev)
        q_copy.start()
        q_copy.wait_send()
        src = w_piece(f, c, g)
        w_copy = copy(src, src, sends("out_w"), wz["mate"], mate_dev)
        w_copy.start()
        arrived(w_piece(mate, c, 1 - g), wy["mate"])
        w_to_sub("mate", 1 - g, 1)
        w_copy.wait_send()

        def pi(i):
            src = att_part(attf.at[h], i)
            arrived(src, ra + i)
            copy(src, src, sends("ax", PIECES) + i, rx + i, x_dev).start()
            arrived(w_part(peer_in, c, g, i), wz["pi"] + i)
            w_part_to_y("pi", i)

        each_part(pi)
        w_to_sub("pi", g, 0)

        def po(i):
            arrived(w_part(peer_out, c, g, i), wz["po"] + i)
            w_part_to_y("po", i)

        each_part(po)

    w_to_sub("po", g, 0)
    each_part(lambda i: arrived(w_part(peer_in, c, 1 - g, i), wy["pi"] + i))
    w_to_sub("pi", 1 - g, 1)
    each_part(lambda i: arrived(att_part(attf.at[1 - h], i), rx + i))
    arrived(w_shard(f, 1 - c), ws_own)
    for b in ("mate", "pi"):
        arrived(w_piece(wblock[b], 1 - c, g), ws[b])
        arrived(w_piece(wblock[b], 1 - c, 1 - g), ws[b] + 1)

    depth = 2 * wrows
    tile = 512

    def product(block, lanes):
        att_lanes = pl.ds(pl.multiple_of((block % 2) * depth, HEAD_DIM), depth)
        return jnp.dot(
            attf[block // 2, :, att_lanes], wf[block, :, lanes], preferred_element_type=jnp.float32
        )

    @pl.loop(0, wide // tile)
    def _(n):
        lanes = pl.ds(pl.multiple_of(n * tile, tile), tile)
        pacc[:, lanes] = product(f, lanes) + product(mate, lanes) + product(peer_in, lanes)

    each_part(lambda i: arrived(w_part(peer_out, c, 1 - g, i), wy["po"] + i))
    w_to_sub("po", 1 - g, 1)
    arrived(w_piece(peer_out, 1 - c, g), ws["po"])
    arrived(w_piece(peer_out, 1 - c, 1 - g), ws["po"] + 1)

    @pl.loop(0, wide // tile)
    def _(n):
        lanes = pl.ds(pl.multiple_of(n * tile, tile), tile)
        total = pacc[:, lanes] + product(peer_out, lanes)
        out[:, lanes] = (total * gate[:, lanes]).astype(jnp.bfloat16)

    def sent(src, name, offset=0):
        copy(src, src, sends(name) + offset, 0, sub_dev).wait_send()

    sent(w, "wown")
    for b in ("mate", "pi", "po"):
        for which in range(2):
            sent(w_piece(0, 0, 0), "wsub" + b + str(which))
    sent(w_piece(0, 0, 0), "wypmate")

    def common_sent(i):
        sent(att_part(aout, 0), "ax", i)
        for b in ("pi", "po"):
            sent(w_part(0, 0, 0, 0), "wyp" + b, i)

    each_part(common_sent)

    @pl.when(inner)
    def _():
        for n in "kv":
            for name in ("i_sub", "i_peer", "o_peer", "o_sub", "pi_sub", "po_sub"):
                sent(k, name + n)
        sent(w_piece(0, 0, 0), "w_in_out")

        def inner_sent(i):
            sent(att_part(aout, 0), "aout", i)
            for name in ("w_own_peer", "w_mate_peer", "woutpi", "woutpo"):
                sent(w_part(0, 0, 0, 0), name, i)

        each_part(inner_sent)

    assert sends.used <= send_sems.shape[0] and recvs.used <= recv_sems.shape[0]


def line_shards(
    queries, keys, values, out_weight, time_table, action_table, levels, actions, cycle_order
):
    gate_row = gate_of_slot(time_table, action_table, levels, actions)
    rows, cols = queries.shape
    wrows, wide = out_weight.shape
    heads = cols // HEAD_DIM
    bf16, f32 = jnp.bfloat16, jnp.float32
    vmem = pl.BlockSpec(memory_space=pltpu.VMEM)
    return pl.pallas_call(
        line_kernel,
        out_shape=jax.ShapeDtypeStruct((rows, wide), bf16),
        in_specs=[pl.BlockSpec(memory_space=pltpu.SMEM)] + [vmem] * 5,
        out_specs=vmem,
        scratch_shapes=[
            pltpu.VMEM((4, 2 * rows, cols), bf16),
            pltpu.VMEM((4, 2 * rows, cols), bf16),
            pltpu.VMEM((2, rows, cols), bf16),
            pltpu.VMEM((2 * heads, rows, HEAD_DIM), f32),
            pltpu.VMEM((2 * heads, rows, HEAD_DIM), f32),
            pltpu.VMEM((2, rows, cols), bf16),
            pltpu.VMEM((rows, cols), bf16),
            pltpu.VMEM((4, 2 * wrows, wide), bf16),
            pltpu.VMEM((rows, wide), f32),
            pltpu.SemaphoreType.DMA((80,)),
            pltpu.SemaphoreType.DMA((80,)),
            pltpu.SemaphoreType.DMA((4,)),
        ],
        compiler_params=pltpu.CompilerParams(
            collective_id=0, has_side_effects=True, vmem_limit_bytes=62 * 1024 * 1024
        ),
    )(cycle_order, queries, keys, values, out_weight, gate_row)


def solution(mesh):
    in_specs = (
        P(("group", "frame", "sub"), "head"),
        P(("group", "frame", "sub"), "head"),
        P(("group", "frame", "sub"), "head"),
        P(("frame", "sub"), "head"),
        P(None, "head"),
        P(None, "head"),
        P("group"),
        P("group", None),
        P("group"),
    )
    out_specs = P(("group", "frame", "sub"), "head")
    in_line = all(mesh.shape[a] == n for a, n in (("group", 2), ("frame", 4), ("head", 2), ("sub", 2)))
    shards = line_shards if in_line else ring_shards
    return jax.shard_map(shards, mesh=mesh, in_specs=in_specs, out_specs=out_specs, check_vma=False)
```

```python
import functools

import jax
import jax.numpy as jnp
from jax import lax
from jax.experimental import pallas as pl
from jax.experimental.pallas import tpu as pltpu
from jax.sharding import PartitionSpec as P

HEAD_DIM = 128
LEVELS = 50
ACTIONS = 256
FWIN = 3
PIECES = 5
AHEAD = 2
ROW_PARTS = 10
W_AHEAD = 2 * AHEAD
LOG2E = 1.4426950408889634
MESH = pl.DeviceIdType.MESH


def from_behind(array, axis, by):
    count = lax.axis_size(axis)
    return lax.ppermute(array, axis, [(i, (i + by) % count) for i in range(count)])


def attend_heads(query_rows, key_rows, value_rows, key_valid):
    query_count = query_rows.shape[0]
    length = key_rows.shape[0]
    row_width = query_rows.shape[1]
    head_count = row_width // HEAD_DIM
    query_heads = jnp.moveaxis(query_rows.reshape(query_count, head_count, HEAD_DIM), 1, 0)
    key_heads = jnp.moveaxis(key_rows.reshape(length, head_count, HEAD_DIM), 1, 0)
    value_heads = jnp.moveaxis(value_rows.reshape(length, head_count, HEAD_DIM), 1, 0)
    factor = HEAD_DIM ** (-0.5)

    def one_head(operands):
        query_one, key_one, value_one = operands
        scores = jnp.dot(query_one, key_one.T, preferred_element_type=jnp.float32) * factor
        scores = jnp.where(key_valid[None, :], scores, -1e30)
        largest = jnp.max(scores, axis=1, keepdims=True)
        weights = jnp.exp(scores - largest)
        totals = jnp.sum(weights, axis=1, keepdims=True)
        mixed_rows = jnp.dot(
            weights.astype(jnp.bfloat16), value_one, preferred_element_type=jnp.float32
        )
        return (mixed_rows / totals).astype(jnp.bfloat16)

    result = lax.map(one_head, (query_heads, key_heads, value_heads))
    return jnp.moveaxis(result, 0, 1).reshape(query_count, row_width)


def gate_of_slot(time_table, action_table, levels, actions):
    frame_slot = lax.axis_index("frame")
    level_onehot = (jnp.arange(LEVELS, dtype=jnp.int32) == levels[frame_slot]).astype(jnp.bfloat16)
    action_match = jnp.arange(ACTIONS, dtype=jnp.int32)[None, :] == actions[frame_slot][:, None]
    action_count = jnp.sum(action_match.astype(jnp.float32), axis=0).astype(jnp.bfloat16)
    gate_row = jnp.dot(level_onehot[None, :], time_table, preferred_element_type=jnp.float32)
    return gate_row + jnp.dot(
        action_count[None, :], action_table, preferred_element_type=jnp.float32
    )


def ring_shards(
    queries, keys, values, out_weight, time_table, action_table, levels, actions, cycle_order
):
    window = FWIN
    own_position = cycle_order[lax.axis_index("frame")]
    gate_row = gate_of_slot(time_table, action_table, levels, actions)
    paired = jnp.stack([keys, values])
    block_rows = paired.shape[1] * lax.axis_size("sub")
    local_pair = lax.all_gather(paired, "sub", axis=1, tiled=True)
    blocks = [local_pair]
    for distance in range(1, window):
        blocks.append(from_behind(local_pair, "frame", distance))
    joined = jnp.concatenate(blocks, axis=1)
    block_valid = own_position >= jnp.arange(window, dtype=jnp.int32)
    key_valid = jnp.repeat(block_valid, block_rows)
    attended = attend_heads(queries, joined[0], joined[1], key_valid)
    outputs = lax.all_gather(attended, "head", axis=1, tiled=True)
    all_rows = lax.all_gather(out_weight, ("frame", "sub"), axis=0, tiled=True)
    projected = jnp.dot(outputs, all_rows, preferred_element_type=jnp.float32)
    return (gate_row * projected).astype(jnp.bfloat16)


class Indices:
    def __init__(self, sems):
        self.sems, self.names, self.used = sems, {}, 0

    def __call__(self, name, count=1):
        if name not in self.names:
            self.names[name] = (self.used, count)
            self.used += count
        return self.names[name][0]


def line_kernel(
    cycle, levels, actions, q, k, v, w, time_table, action_table, out,
    kb, vb, qb, stat, acc, attf, aout, wf, pacc, gate, send_sems, recv_sems, local_sems,
):
    rows, cols = q.shape
    wrows, wide = w.shape
    half = wrows // 2
    part = half // ROW_PARTS
    heads = cols // HEAD_DIM
    per = heads // PIECES
    att_cols = per * HEAD_DIM
    tile = 512
    scale = HEAD_DIM ** (-0.5) * LOG2E

    g, f, h, c = (lax.axis_index(name) for name in ("group", "frame", "head", "sub"))
    side = f // 2
    f_in, f_out = 1 + side, 3 * side
    peer_in, peer_out = 2 - side, 3 - 3 * side
    inner = f == f_in
    mate = f_in + f_out - f
    sub_dev = (g, f, h, 1 - c)
    x_dev = (g, f, 1 - h, c)
    y_dev = (1 - g, f, h, c)
    mate_dev = (g, mate, h, c)
    peer_dev = (g, peer_in, h, c)

    barrier = pltpu.get_barrier_semaphore()
    for dev in (sub_dev, x_dev, y_dev, mate_dev):
        pl.semaphore_signal(barrier, inc=1, device_id=dev, device_id_type=MESH)

    @pl.when(inner)
    def _():
        pl.semaphore_signal(barrier, inc=1, device_id=peer_dev, device_id_type=MESH)
        pl.semaphore_wait(barrier, 5)

    @pl.when(jnp.logical_not(inner))
    def _():
        pl.semaphore_wait(barrier, 4)

    sends, recvs = Indices(send_sems), Indices(recv_sems)

    def copy(src, dst, send, recv, dev):
        return pltpu.make_async_remote_copy(
            src_ref=src,
            dst_ref=dst,
            send_sem=send_sems.at[send],
            recv_sem=recv_sems.at[recv],
            device_id=dev,
            device_id_type=MESH,
        )

    def arrived(dst, recv):
        copy(dst, dst, 0, recv, sub_dev).wait_recv()

    def own_rows(base, count, index):
        return pl.ds(pl.multiple_of(base + index * count, 16), count)

    def kv_half(buf, block, cc):
        return buf.at[block, own_rows(0, rows, cc), :]

    def kv_part(buf, block, cc, i):
        lanes = pl.ds(pl.multiple_of(i * att_cols, HEAD_DIM), att_cols)
        return buf.at[block, own_rows(0, rows, cc), lanes]

    def w_shard(block, cc):
        return wf.at[block, own_rows(0, wrows, cc), :]

    def w_piece(block, cc, gg):
        return wf.at[block, own_rows(cc * wrows, half, gg), :]

    def w_part(block, cc, gg, i):
        return wf.at[block, own_rows(cc * wrows + gg * half, part, i), :]

    def att_part(ref, i):
        return ref.at[:, pl.ds(pl.multiple_of(i * att_cols, HEAD_DIM), att_cols)]

    kv_z = lambda n, which: recvs("kvz" + n + which, 1 if which == "pi" else PIECES)
    kv_s = lambda n, which: recvs("kvs" + n + which, 1 if which in ("i", "pi") else PIECES)
    wz = {b: recvs("wz" + b, ROW_PARTS if b == "po" else 1) for b in ("mate", "pi", "po")}
    wy = {b: recvs("wy" + b, ROW_PARTS if b == "po" else 1) for b in ("mate", "pi", "po")}
    ws = {b: recvs("ws" + b, 2) for b in ("mate", "pi", "po")}
    ws_own, rq = recvs("wsown"), recvs("q")
    ra, rx = recvs("ra", PIECES), recvs("rx", PIECES)
    wblock = {"mate": mate, "pi": peer_in, "po": peer_out}

    def w_to_sub(b, gg, which):
        src = w_piece(wblock[b], c, gg)
        one = copy(src, src, sends("wsub" + b + str(which)), ws[b] + which, sub_dev)
        one.start()

    def w_piece_to_y(b):
        src = w_piece(wblock[b], c, g)
        copy(src, src, sends("wy" + b), wy[b], y_dev).start()

    def last_w_to_y(i):
        src = w_part(peer_out, c, g, i)
        copy(src, src, sends("wypo", ROW_PARTS) + i, wy["po"] + i, y_dev).start()

    def last_w_to_mate(i):
        src = w_part(peer_out, c, g, i)
        copy(src, src, sends("wout", ROW_PARTS) + i, wz["po"] + i, mate_dev).start()

    def mate_w_to_peer(i):
        src = w_part(mate, c, g, i)
        copy(src, src, sends("w_mate_peer", ROW_PARTS) + i, wz["po"] + i, peer_dev).start()

    def gate_rows():
        @pl.loop(0, wide // tile)
        def _(n):
            lanes = pl.ds(pl.multiple_of(n * tile, tile), tile)
            level_rows = time_table[:, lanes].astype(jnp.float32)
            level_at = lax.broadcasted_iota(jnp.int32, level_rows.shape, 0)
            total = jnp.sum(
                jnp.where(level_at == levels[f], level_rows, 0.0), axis=0, keepdims=True
            )
            action_rows = action_table[:, lanes].astype(jnp.float32)
            action_at = lax.broadcasted_iota(jnp.int32, action_rows.shape, 0)
            times = jnp.zeros(action_rows.shape, jnp.float32)
            for a in range(actions.shape[1]):
                times += (action_at == actions[f, a]).astype(jnp.float32)
            gate[:, lanes] = total + jnp.sum(times * action_rows, axis=0, keepdims=True)

    def valid_of(slot, block):
        distance = (slot - block + 4) % 4
        return cycle[block] == cycle[slot] - distance

    def unit(si, block, head, finish=None):
        slot = jnp.where(si == 0, f_in, f_out)
        valid = valid_of(slot, block)
        lanes = pl.ds(pl.multiple_of(head * HEAD_DIM, HEAD_DIM), HEAD_DIM)
        si_head = si * heads + head
        scores = lax.dot_general(
            qb[si, :, lanes], kb[block, :, lanes], (((1,), (1,)), ((), ())),
            preferred_element_type=jnp.float32,
        )
        old = stat[si_head]
        old_max, old_total = old[:, :1], old[:, 64:65]
        block_max = jnp.where(valid, jnp.max(scores, axis=1, keepdims=True), -1e30)
        new_max = jnp.maximum(old_max, block_max)
        weights = jnp.exp2((scores - jnp.where(valid, new_max, 1e30)) * scale)
        fade = jnp.exp2((old_max - new_max) * scale)
        total = old_total * fade + jnp.sum(weights, axis=1, keepdims=True)
        mixed = acc[si_head] * fade + jnp.dot(
            weights.astype(jnp.bfloat16), vb[block, :, lanes], preferred_element_type=jnp.float32
        )
        if finish is None:
            acc[si_head] = mixed
            lane = lax.broadcasted_iota(jnp.int32, (rows, HEAD_DIM), 1)
            stat[si_head] = jnp.where(lane < 64, new_max, total)
        else:
            finish[:, lanes] = (mixed / total).astype(jnp.bfloat16)

    def units(si, block):
        @pl.loop(0, heads)
        def _(head):
            unit(si, block, head)

    def each_part(body):
        @pl.loop(0, PIECES)
        def _(i):
            body(i)

    own_w = pltpu.make_async_copy(w, w_shard(f, c), local_sems.at[0])
    own_w.start()
    w_to_partner = copy(w, w_shard(f, c), sends("wown"), ws_own, sub_dev)

    @pl.when(inner)
    def _():
        for n, ref, buf in (("k", k, kb), ("v", v, vb)):
            copy(ref, kv_half(buf, f, c), sends("i_sub" + n), kv_s(n, "i"), sub_dev).start()
            copy(ref, kv_half(buf, f, c), sends("i_peer" + n), kv_z(n, "pi"), peer_dev).start()
        locals_ = [
            pltpu.make_async_copy(k, kv_half(kb, f, c), local_sems.at[1]),
            pltpu.make_async_copy(v, kv_half(vb, f, c), local_sems.at[2]),
            pltpu.make_async_copy(q, qb.at[0], local_sems.at[3]),
        ]
        for one in locals_:
            one.start()
        w_to_partner.start()
        copy(
            w.at[own_rows(0, half, g), :], w_piece(f, c, g), sends("w_in_out"), wz["mate"], mate_dev
        ).start()

        @pl.loop(0, 2 * heads)
        def _(i):
            acc[i] = jnp.zeros((rows, HEAD_DIM), jnp.float32)
            lane = lax.broadcasted_iota(jnp.int32, (rows, HEAD_DIM), 1)
            stat[i] = jnp.where(lane < 64, -1e30, 0.0)

        gate_rows()

        for one in locals_:
            one.wait()
        for n, buf in (("k", kb), ("v", vb)):
            arrived(kv_half(buf, f, 1 - c), kv_s(n, "i"))
        units(0, f_in)
        own_w.wait()

        def relay(i):
            for n, buf in (("k", kb), ("v", vb)):
                src = kv_part(buf, f_out, c, i)
                arrived(src, kv_z(n, "o") + i)
                send = sends("o_peer" + n, PIECES) + i
                copy(src, src, send, kv_z(n, "po") + i, peer_dev).start()
                copy(src, src, sends("o_sub" + n, PIECES) + i, kv_s(n, "o") + i, sub_dev).start()

        src = w_piece(f, c, g)
        copy(src, src, sends("w_own_peer"), wz["pi"], peer_dev).start()
        for i in range(AHEAD):
            relay(i)
        for n, buf in (("k", kb), ("v", vb)):
            src = kv_half(buf, peer_in, c)
            arrived(src, kv_z(n, "pi"))
            copy(src, src, sends("pi_sub" + n), kv_s(n, "pi"), sub_dev).start()
        arrived(qb.at[1], rq)
        for n, buf in (("k", kb), ("v", vb)):
            arrived(kv_half(buf, peer_in, 1 - c), kv_s(n, "pi"))
        units(1, peer_in)
        arrived(w_piece(peer_in, c, g), wz["pi"])
        src = w_piece(peer_in, c, g)
        copy(src, src, sends("w_pi_out"), wz["pi"], mate_dev).start()
        w_piece_to_y("pi")
        w_to_sub("pi", g, 0)
        next_block = jnp.where(side == 0, f_out, peer_in)
        last_block = jnp.where(side == 0, peer_out, f_in)

        def last(i):
            @pl.when(i + AHEAD < PIECES)
            def _():
                relay(i + AHEAD)

            @pl.when(i + AHEAD == PIECES)
            def _():
                arrived(w_piece(mate, c, g), wz["mate"])
                w_piece_to_y("mate")
                w_to_sub("mate", g, 0)

            @pl.when(i + AHEAD >= PIECES)
            def _():
                for j in range(2):
                    mate_w_to_peer(2 * (i + AHEAD - PIECES) + j)

            for n, buf in (("k", kb), ("v", vb)):
                src = kv_part(buf, peer_out, c, i)
                arrived(src, kv_z(n, "po") + i)
                copy(src, src, sends("po_sub" + n, PIECES) + i, kv_s(n, "po") + i, sub_dev).start()
            for n, buf in (("k", kb), ("v", vb)):
                arrived(kv_part(buf, f_out, 1 - c, i), kv_s(n, "o") + i)

            @pl.loop(0, per)
            def _(j):
                unit(1, f_out, i * per + j)
                unit(0, next_block, i * per + j)

            for n, buf in (("k", kb), ("v", vb)):
                arrived(kv_part(buf, peer_out, 1 - c, i), kv_s(n, "po") + i)

            @pl.loop(0, per)
            def _(j):
                unit(1, last_block, i * per + j, aout)
                unit(0, peer_out, i * per + j, attf.at[h])

            src = att_part(aout, i)
            copy(src, att_part(attf.at[h], i), sends("aout", PIECES) + i, ra + i, mate_dev).start()
            src = att_part(attf.at[h], i)
            copy(src, src, sends("ax", PIECES) + i, rx + i, x_dev).start()

        each_part(last)
        arrived(w_piece(mate, c, 1 - g), wy["mate"])
        w_to_sub("mate", 1 - g, 1)

    @pl.when(jnp.logical_not(inner))
    def _():
        def kv_out(i):
            lanes = pl.ds(pl.multiple_of(i * att_cols, HEAD_DIM), att_cols)
            return [
                copy(
                    ref.at[:, lanes], kv_part(buf, f, c, i), sends("out_" + n, PIECES) + i,
                    kv_z(n, "o") + i, mate_dev,
                )
                for n, ref, buf in (("k", k, kb), ("v", v, vb))
            ]

        def kv_start(i):
            for one in kv_out(i):
                one.start()

        def kv_sent(i):
            for one in kv_out(i):
                one.wait_send()

        q_copy = copy(q, qb.at[1], sends("out_q"), rq, mate_dev)
        q_copy.start()
        kv_start(0)
        w_to_partner.start()
        own_w.wait()
        arrived(w_piece(mate, c, g), wz["mate"])
        w_piece_to_y("mate")
        w_to_sub("mate", g, 0)
        q_copy.wait_send()

        @pl.loop(1, PIECES)
        def _(i):
            kv_start(i)
            kv_sent(i - 1)

        src = w_piece(f, c, g)
        w_copy = copy(src, src, sends("out_w"), wz["mate"], mate_dev)
        w_copy.start()
        kv_sent(PIECES - 1)
        gate_rows()
        arrived(w_piece(mate, c, 1 - g), wy["mate"])
        w_to_sub("mate", 1 - g, 1)
        arrived(w_piece(peer_in, c, g), wz["pi"])
        w_piece_to_y("pi")
        w_to_sub("pi", g, 0)
        w_copy.wait_send()

        def back(i):
            src = att_part(attf.at[h], i)
            arrived(src, ra + i)
            copy(src, src, sends("ax", PIECES) + i, rx + i, x_dev).start()

        each_part(back)

    def last_w(i):
        @pl.when(inner & (i + W_AHEAD < ROW_PARTS))
        def _():
            mate_w_to_peer(i + W_AHEAD)

        arrived(w_part(peer_out, c, g, i), wz["po"] + i)

        @pl.when(inner)
        def _():
            last_w_to_mate(i)

        last_w_to_y(i)

    depth = 2 * wrows

    def product(block, lanes):
        att_lanes = pl.ds(pl.multiple_of((block % 2) * depth, HEAD_DIM), depth)
        return jnp.dot(
            attf[block // 2, :, att_lanes], wf[block, :, lanes], preferred_element_type=jnp.float32
        )

    tiles = wide // tile
    early = ROW_PARTS - tiles

    @pl.loop(0, early)
    def _(i):
        last_w(i)

    arrived(w_piece(peer_in, c, 1 - g), wy["pi"])
    w_to_sub("pi", 1 - g, 1)
    each_part(lambda i: arrived(att_part(attf.at[1 - h], i), rx + i))
    arrived(w_shard(f, 1 - c), ws_own)
    for b in ("mate", "pi"):
        arrived(w_piece(wblock[b], 1 - c, g), ws[b])
        arrived(w_piece(wblock[b], 1 - c, 1 - g), ws[b] + 1)

    @pl.loop(0, tiles)
    def _(n):
        last_w(n + early)
        lanes = pl.ds(pl.multiple_of(n * tile, tile), tile)
        pacc[:, lanes] = product(f, lanes) + product(mate, lanes) + product(peer_in, lanes)

    w_to_sub("po", g, 0)

    @pl.loop(0, ROW_PARTS)
    def _(i):
        arrived(w_part(peer_out, c, 1 - g, i), wy["po"] + i)

    w_to_sub("po", 1 - g, 1)
    arrived(w_piece(peer_out, 1 - c, g), ws["po"])
    arrived(w_piece(peer_out, 1 - c, 1 - g), ws["po"] + 1)

    @pl.loop(0, tiles)
    def _(n):
        lanes = pl.ds(pl.multiple_of(n * tile, tile), tile)
        total = pacc[:, lanes] + product(peer_out, lanes)
        out[:, lanes] = (total * gate[:, lanes]).astype(jnp.bfloat16)

    def sent(src, name, offset=0):
        copy(src, src, sends(name) + offset, 0, sub_dev).wait_send()

    sent(w, "wown")
    for b in ("mate", "pi", "po"):
        for which in range(2):
            sent(w_piece(0, 0, 0), "wsub" + b + str(which))
    sent(w_piece(0, 0, 0), "wymate")
    sent(w_piece(0, 0, 0), "wypi")

    def common_sent(i):
        sent(att_part(aout, 0), "ax", i)

    each_part(common_sent)

    @pl.loop(0, ROW_PARTS)
    def _(i):
        sent(w_part(0, 0, 0, 0), "wypo", i)

    @pl.when(inner)
    def _():
        for n in "kv":
            for name in ("i_sub", "i_peer", "pi_sub"):
                sent(k, name + n)
        for name in ("w_in_out", "w_own_peer", "w_pi_out"):
            sent(w_piece(0, 0, 0), name)

        def inner_sent(i):
            sent(att_part(aout, 0), "aout", i)
            for name in ("o_peerk", "o_subk", "po_subk", "o_peerv", "o_subv", "po_subv"):
                sent(att_part(aout, 0), name, i)

        each_part(inner_sent)

        @pl.loop(0, ROW_PARTS)
        def _(i):
            for name in ("w_mate_peer", "wout"):
                sent(w_part(0, 0, 0, 0), name, i)

    assert sends.used <= send_sems.shape[0] and recvs.used <= recv_sems.shape[0]


def line_shards(
    queries, keys, values, out_weight, time_table, action_table, levels, actions, cycle_order
):
    rows, cols = queries.shape
    wrows, wide = out_weight.shape
    heads = cols // HEAD_DIM
    bf16, f32 = jnp.bfloat16, jnp.float32
    vmem, smem, anywhere = (
        pl.BlockSpec(memory_space=space) for space in (pltpu.VMEM, pltpu.SMEM, pl.ANY)
    )
    return pl.pallas_call(
        line_kernel,
        out_shape=jax.ShapeDtypeStruct((rows, wide), bf16),
        in_specs=[smem] * 3 + [anywhere] * 4 + [vmem] * 2,
        out_specs=vmem,
        scratch_shapes=[
            pltpu.VMEM((4, 2 * rows, cols), bf16),
            pltpu.VMEM((4, 2 * rows, cols), bf16),
            pltpu.VMEM((2, rows, cols), bf16),
            pltpu.VMEM((2 * heads, rows, HEAD_DIM), f32),
            pltpu.VMEM((2 * heads, rows, HEAD_DIM), f32),
            pltpu.VMEM((2, rows, cols), bf16),
            pltpu.VMEM((rows, cols), bf16),
            pltpu.VMEM((4, 2 * wrows, wide), bf16),
            pltpu.VMEM((rows, wide), f32),
            pltpu.VMEM((1, wide), f32),
            pltpu.SemaphoreType.DMA((120,)),
            pltpu.SemaphoreType.DMA((120,)),
            pltpu.SemaphoreType.DMA((4,)),
        ],
        compiler_params=pltpu.CompilerParams(
            collective_id=0, has_side_effects=True, vmem_limit_bytes=62 * 1024 * 1024
        ),
    )(
        cycle_order, levels, actions, queries, keys, values, out_weight, time_table, action_table
    )


def solution(mesh):
    in_specs = (
        P(("group", "frame", "sub"), "head"),
        P(("group", "frame", "sub"), "head"),
        P(("group", "frame", "sub"), "head"),
        P(("frame", "sub"), "head"),
        P(None, "head"),
        P(None, "head"),
        P("group"),
        P("group", None),
        P("group"),
    )
    out_specs = P(("group", "frame", "sub"), "head")
    in_line = all(mesh.shape[a] == n for a, n in (("group", 2), ("frame", 4), ("head", 2), ("sub", 2)))
    shards = line_shards if in_line else ring_shards
    return jax.shard_map(shards, mesh=mesh, in_specs=in_specs, out_specs=out_specs, check_vma=False)
```

```python
import functools

import jax
import jax.numpy as jnp
from jax import lax
from jax.experimental import pallas as pl
from jax.experimental.pallas import tpu as pltpu
from jax.sharding import PartitionSpec as P

HEAD_DIM = 128
LEVELS = 50
ACTIONS = 256
FWIN = 3
PIECES = 5
AHEAD = 2
ROW_PARTS = 10
W_AHEAD = 2 * AHEAD
GANG = 2
LOG2E = 1.4426950408889634
MESH = pl.DeviceIdType.MESH


def from_behind(array, axis, by):
    count = lax.axis_size(axis)
    return lax.ppermute(array, axis, [(i, (i + by) % count) for i in range(count)])


def attend_heads(query_rows, key_rows, value_rows, key_valid):
    query_count = query_rows.shape[0]
    length = key_rows.shape[0]
    row_width = query_rows.shape[1]
    head_count = row_width // HEAD_DIM
    query_heads = jnp.moveaxis(query_rows.reshape(query_count, head_count, HEAD_DIM), 1, 0)
    key_heads = jnp.moveaxis(key_rows.reshape(length, head_count, HEAD_DIM), 1, 0)
    value_heads = jnp.moveaxis(value_rows.reshape(length, head_count, HEAD_DIM), 1, 0)
    factor = HEAD_DIM ** (-0.5)

    def one_head(operands):
        query_one, key_one, value_one = operands
        scores = jnp.dot(query_one, key_one.T, preferred_element_type=jnp.float32) * factor
        scores = jnp.where(key_valid[None, :], scores, -1e30)
        largest = jnp.max(scores, axis=1, keepdims=True)
        weights = jnp.exp(scores - largest)
        totals = jnp.sum(weights, axis=1, keepdims=True)
        mixed_rows = jnp.dot(
            weights.astype(jnp.bfloat16), value_one, preferred_element_type=jnp.float32
        )
        return (mixed_rows / totals).astype(jnp.bfloat16)

    result = lax.map(one_head, (query_heads, key_heads, value_heads))
    return jnp.moveaxis(result, 0, 1).reshape(query_count, row_width)


def gate_of_slot(time_table, action_table, levels, actions):
    frame_slot = lax.axis_index("frame")
    level_onehot = (jnp.arange(LEVELS, dtype=jnp.int32) == levels[frame_slot]).astype(jnp.bfloat16)
    action_match = jnp.arange(ACTIONS, dtype=jnp.int32)[None, :] == actions[frame_slot][:, None]
    action_count = jnp.sum(action_match.astype(jnp.float32), axis=0).astype(jnp.bfloat16)
    gate_row = jnp.dot(level_onehot[None, :], time_table, preferred_element_type=jnp.float32)
    return gate_row + jnp.dot(
        action_count[None, :], action_table, preferred_element_type=jnp.float32
    )


def ring_shards(
    queries, keys, values, out_weight, time_table, action_table, levels, actions, cycle_order
):
    window = FWIN
    own_position = cycle_order[lax.axis_index("frame")]
    gate_row = gate_of_slot(time_table, action_table, levels, actions)
    paired = jnp.stack([keys, values])
    block_rows = paired.shape[1] * lax.axis_size("sub")
    local_pair = lax.all_gather(paired, "sub", axis=1, tiled=True)
    blocks = [local_pair]
    for distance in range(1, window):
        blocks.append(from_behind(local_pair, "frame", distance))
    joined = jnp.concatenate(blocks, axis=1)
    block_valid = own_position >= jnp.arange(window, dtype=jnp.int32)
    key_valid = jnp.repeat(block_valid, block_rows)
    attended = attend_heads(queries, joined[0], joined[1], key_valid)
    outputs = lax.all_gather(attended, "head", axis=1, tiled=True)
    all_rows = lax.all_gather(out_weight, ("frame", "sub"), axis=0, tiled=True)
    projected = jnp.dot(outputs, all_rows, preferred_element_type=jnp.float32)
    return (gate_row * projected).astype(jnp.bfloat16)


class Indices:
    def __init__(self, sems):
        self.sems, self.names, self.used = sems, {}, 0

    def __call__(self, name, count=1):
        if name not in self.names:
            self.names[name] = (self.used, count)
            self.used += count
        return self.names[name][0]


def line_kernel(
    cycle, levels, actions, q, k, v, w, time_table, action_table, out,
    kb, vb, qb, stat, acc, attf, aout, wf, pacc, gate, send_sems, recv_sems, local_sems,
):
    rows, cols = q.shape
    wrows, wide = w.shape
    half = wrows // 2
    part = half // ROW_PARTS
    heads = cols // HEAD_DIM
    per = heads // PIECES
    att_cols = per * HEAD_DIM
    tile = 512
    keys_n = 2 * rows
    scale = HEAD_DIM ** (-0.5) * LOG2E

    g, f, h, c = (lax.axis_index(name) for name in ("group", "frame", "head", "sub"))
    side = f // 2
    f_in, f_out = 1 + side, 3 * side
    peer_in, peer_out = 2 - side, 3 - 3 * side
    inner = f == f_in
    mate = f_in + f_out - f
    sub_dev = (g, f, h, 1 - c)
    x_dev = (g, f, 1 - h, c)
    y_dev = (1 - g, f, h, c)
    mate_dev = (g, mate, h, c)
    peer_dev = (g, peer_in, h, c)

    barrier = pltpu.get_barrier_semaphore()
    for dev in (sub_dev, x_dev, y_dev, mate_dev):
        pl.semaphore_signal(barrier, inc=1, device_id=dev, device_id_type=MESH)

    @pl.when(inner)
    def _():
        pl.semaphore_signal(barrier, inc=1, device_id=peer_dev, device_id_type=MESH)
        pl.semaphore_wait(barrier, 5)

    @pl.when(jnp.logical_not(inner))
    def _():
        pl.semaphore_wait(barrier, 4)

    sends, recvs = Indices(send_sems), Indices(recv_sems)

    def copy(src, dst, send, recv, dev):
        return pltpu.make_async_remote_copy(
            src_ref=src,
            dst_ref=dst,
            send_sem=send_sems.at[send],
            recv_sem=recv_sems.at[recv],
            device_id=dev,
            device_id_type=MESH,
        )

    def arrived(dst, recv):
        copy(dst, dst, 0, recv, sub_dev).wait_recv()

    def own_rows(base, count, index):
        return pl.ds(pl.multiple_of(base + index * count, 16), count)

    def kv_half(buf, block, cc):
        return buf.at[block, own_rows(0, rows, cc), :]

    def kv_part(buf, block, cc, i):
        lanes = pl.ds(pl.multiple_of(i * att_cols, HEAD_DIM), att_cols)
        return buf.at[block, own_rows(0, rows, cc), lanes]

    def w_shard(block, cc):
        return wf.at[block, own_rows(0, wrows, cc), :]

    def w_piece(block, cc, gg):
        return wf.at[block, own_rows(cc * wrows, half, gg), :]

    def w_part(block, cc, gg, i):
        return wf.at[block, own_rows(cc * wrows + gg * half, part, i), :]

    def att_part(ref, i):
        return ref.at[:, pl.ds(pl.multiple_of(i * att_cols, HEAD_DIM), att_cols)]

    kv_z = lambda n, which: recvs("kvz" + n + which, 1 if which == "pi" else PIECES)
    kv_s = lambda n, which: recvs("kvs" + n + which, 1 if which in ("i", "pi") else PIECES)
    wz = {b: recvs("wz" + b, ROW_PARTS if b == "po" else 1) for b in ("mate", "pi", "po")}
    wy = {b: recvs("wy" + b, ROW_PARTS if b == "po" else 1) for b in ("mate", "pi", "po")}
    ws = {b: recvs("ws" + b, 2) for b in ("mate", "pi", "po")}
    ws_own, rq = recvs("wsown"), recvs("q")
    ra, rx = recvs("ra", PIECES), recvs("rx", PIECES)
    wblock = {"mate": mate, "pi": peer_in, "po": peer_out}

    def w_to_sub(b, gg, which):
        src = w_piece(wblock[b], c, gg)
        one = copy(src, src, sends("wsub" + b + str(which)), ws[b] + which, sub_dev)
        one.start()

    def w_piece_to_y(b):
        src = w_piece(wblock[b], c, g)
        copy(src, src, sends("wy" + b), wy[b], y_dev).start()

    def last_w_to_y(i):
        src = w_part(peer_out, c, g, i)
        copy(src, src, sends("wypo", ROW_PARTS) + i, wy["po"] + i, y_dev).start()

    def last_w_to_mate(i):
        src = w_part(peer_out, c, g, i)
        copy(src, src, sends("wout", ROW_PARTS) + i, wz["po"] + i, mate_dev).start()

    def mate_w_to_peer(i):
        src = w_part(mate, c, g, i)
        copy(src, src, sends("w_mate_peer", ROW_PARTS) + i, wz["po"] + i, peer_dev).start()

    def gate_rows():
        @pl.loop(0, wide // tile)
        def _(n):
            lanes = pl.ds(pl.multiple_of(n * tile, tile), tile)
            level_rows = time_table[:, lanes].astype(jnp.float32)
            level_at = lax.broadcasted_iota(jnp.int32, level_rows.shape, 0)
            total = jnp.sum(
                jnp.where(level_at == levels[f], level_rows, 0.0), axis=0, keepdims=True
            )
            action_rows = action_table[:, lanes].astype(jnp.float32)
            action_at = lax.broadcasted_iota(jnp.int32, action_rows.shape, 0)
            times = jnp.zeros(action_rows.shape, jnp.float32)
            for a in range(actions.shape[1]):
                times += (action_at == actions[f, a]).astype(jnp.float32)
            gate[:, lanes] = total + jnp.sum(times * action_rows, axis=0, keepdims=True)

    def valid_of(slot, block):
        distance = (slot - block + 4) % 4
        return cycle[block] == cycle[slot] - distance

    def attend(items):
        lanes = [
            pl.ds(pl.multiple_of(head * HEAD_DIM, HEAD_DIM), HEAD_DIM) for _, _, head, _ in items
        ]
        scores = [
            lax.dot_general(
                qb[si, :, at], kb[block, :, at], (((1,), (1,)), ((), ())),
                preferred_element_type=jnp.float32,
            )
            for (si, block, _, _), at in zip(items, lanes)
        ]
        ones = jnp.ones((keys_n, HEAD_DIM), jnp.bfloat16)
        results = []
        for (si, block, head, _), at, score in zip(items, lanes, scores):
            valid = valid_of(jnp.where(si == 0, f_in, f_out), block)
            old_max = stat[si * heads + head]
            block_max = jnp.where(valid, jnp.max(score, axis=1, keepdims=True), -1e30)
            new_max = jnp.maximum(old_max, block_max)
            base = jnp.where(valid, new_max, 1e30)
            weights = jnp.exp2((score - jnp.concatenate([base] * (keys_n // HEAD_DIM), 1)) * scale)
            fade = jnp.exp2((old_max - new_max) * scale)
            values = jnp.concatenate([vb[block, :, at], ones], 1)
            mixed = jnp.dot(
                weights.astype(jnp.bfloat16), values, preferred_element_type=jnp.float32
            )
            mixed += acc[si * heads + head] * jnp.concatenate([fade, fade], 1)
            results.append((new_max, mixed))
        for (si, _, head, finish), at, (new_max, mixed) in zip(items, lanes, results):
            if finish is None:
                acc[si * heads + head] = mixed
                stat[si * heads + head] = new_max
            else:
                rounded = (mixed[:, :HEAD_DIM] / mixed[:, HEAD_DIM:]).astype(jnp.bfloat16)
                finish[:, at] = rounded

    def units(si, block):
        @pl.loop(0, heads // GANG)
        def _(n):
            attend([(si, block, n * GANG + j, None) for j in range(GANG)])

    def each_part(body):
        @pl.loop(0, PIECES)
        def _(i):
            body(i)

    own_w = pltpu.make_async_copy(w, w_shard(f, c), local_sems.at[0])
    own_w.start()
    w_to_partner = copy(w, w_shard(f, c), sends("wown"), ws_own, sub_dev)

    @pl.when(inner)
    def _():
        for n, ref, buf in (("k", k, kb), ("v", v, vb)):
            copy(ref, kv_half(buf, f, c), sends("i_sub" + n), kv_s(n, "i"), sub_dev).start()
            copy(ref, kv_half(buf, f, c), sends("i_peer" + n), kv_z(n, "pi"), peer_dev).start()
        locals_ = [
            pltpu.make_async_copy(k, kv_half(kb, f, c), local_sems.at[1]),
            pltpu.make_async_copy(v, kv_half(vb, f, c), local_sems.at[2]),
            pltpu.make_async_copy(q, qb.at[0], local_sems.at[3]),
        ]
        for one in locals_:
            one.start()
        w_to_partner.start()
        copy(
            w.at[own_rows(0, half, g), :], w_piece(f, c, g), sends("w_in_out"), wz["mate"], mate_dev
        ).start()

        @pl.loop(0, 2 * heads)
        def _(i):
            acc[i] = jnp.zeros((rows, 2 * HEAD_DIM), jnp.float32)
            stat[i] = jnp.full((rows, HEAD_DIM), -1e30, jnp.float32)

        gate_rows()

        for one in locals_:
            one.wait()
        for n, buf in (("k", kb), ("v", vb)):
            arrived(kv_half(buf, f, 1 - c), kv_s(n, "i"))
        units(0, f_in)
        own_w.wait()

        def relay(i):
            for n, buf in (("k", kb), ("v", vb)):
                src = kv_part(buf, f_out, c, i)
                arrived(src, kv_z(n, "o") + i)
                send = sends("o_peer" + n, PIECES) + i
                copy(src, src, send, kv_z(n, "po") + i, peer_dev).start()
                copy(src, src, sends("o_sub" + n, PIECES) + i, kv_s(n, "o") + i, sub_dev).start()

        src = w_piece(f, c, g)
        copy(src, src, sends("w_own_peer"), wz["pi"], peer_dev).start()
        for i in range(AHEAD):
            relay(i)
        for n, buf in (("k", kb), ("v", vb)):
            src = kv_half(buf, peer_in, c)
            arrived(src, kv_z(n, "pi"))
            copy(src, src, sends("pi_sub" + n), kv_s(n, "pi"), sub_dev).start()
        arrived(qb.at[1], rq)
        for n, buf in (("k", kb), ("v", vb)):
            arrived(kv_half(buf, peer_in, 1 - c), kv_s(n, "pi"))
        units(1, peer_in)
        arrived(w_piece(peer_in, c, g), wz["pi"])
        src = w_piece(peer_in, c, g)
        copy(src, src, sends("w_pi_out"), wz["pi"], mate_dev).start()
        w_piece_to_y("pi")
        w_to_sub("pi", g, 0)
        next_block = jnp.where(side == 0, f_out, peer_in)
        last_block = jnp.where(side == 0, peer_out, f_in)

        def last(i):
            @pl.when(i + AHEAD < PIECES)
            def _():
                relay(i + AHEAD)

            @pl.when(i + AHEAD == PIECES)
            def _():
                arrived(w_piece(mate, c, g), wz["mate"])
                w_piece_to_y("mate")
                w_to_sub("mate", g, 0)

            @pl.when(i + AHEAD >= PIECES)
            def _():
                for j in range(2):
                    mate_w_to_peer(2 * (i + AHEAD - PIECES) + j)

            for n, buf in (("k", kb), ("v", vb)):
                src = kv_part(buf, peer_out, c, i)
                arrived(src, kv_z(n, "po") + i)
                copy(src, src, sends("po_sub" + n, PIECES) + i, kv_s(n, "po") + i, sub_dev).start()
            for n, buf in (("k", kb), ("v", vb)):
                arrived(kv_part(buf, f_out, 1 - c, i), kv_s(n, "o") + i)

            @pl.loop(0, per)
            def _(j):
                head = i * per + j
                attend([(1, f_out, head, None), (0, next_block, head, None)])

            for n, buf in (("k", kb), ("v", vb)):
                arrived(kv_part(buf, peer_out, 1 - c, i), kv_s(n, "po") + i)

            @pl.loop(0, per)
            def _(j):
                head = i * per + j
                attend([(1, last_block, head, aout), (0, peer_out, head, attf.at[h])])

            src = att_part(aout, i)
            copy(src, att_part(attf.at[h], i), sends("aout", PIECES) + i, ra + i, mate_dev).start()
            src = att_part(attf.at[h], i)
            copy(src, src, sends("ax", PIECES) + i, rx + i, x_dev).start()

        each_part(last)
        arrived(w_piece(mate, c, 1 - g), wy["mate"])
        w_to_sub("mate", 1 - g, 1)

    @pl.when(jnp.logical_not(inner))
    def _():
        def kv_out(i):
            lanes = pl.ds(pl.multiple_of(i * att_cols, HEAD_DIM), att_cols)
            return [
                copy(
                    ref.at[:, lanes], kv_part(buf, f, c, i), sends("out_" + n, PIECES) + i,
                    kv_z(n, "o") + i, mate_dev,
                )
                for n, ref, buf in (("k", k, kb), ("v", v, vb))
            ]

        def kv_start(i):
            for one in kv_out(i):
                one.start()

        def kv_sent(i):
            for one in kv_out(i):
                one.wait_send()

        q_copy = copy(q, qb.at[1], sends("out_q"), rq, mate_dev)
        q_copy.start()
        kv_start(0)
        w_to_partner.start()
        own_w.wait()
        arrived(w_piece(mate, c, g), wz["mate"])
        w_piece_to_y("mate")
        w_to_sub("mate", g, 0)
        q_copy.wait_send()

        @pl.loop(1, PIECES)
        def _(i):
            kv_start(i)
            kv_sent(i - 1)

        src = w_piece(f, c, g)
        w_copy = copy(src, src, sends("out_w"), wz["mate"], mate_dev)
        w_copy.start()
        kv_sent(PIECES - 1)
        gate_rows()
        arrived(w_piece(mate, c, 1 - g), wy["mate"])
        w_to_sub("mate", 1 - g, 1)
        arrived(w_piece(peer_in, c, g), wz["pi"])
        w_piece_to_y("pi")
        w_to_sub("pi", g, 0)
        w_copy.wait_send()

        def back(i):
            src = att_part(attf.at[h], i)
            arrived(src, ra + i)
            copy(src, src, sends("ax", PIECES) + i, rx + i, x_dev).start()

        each_part(back)

    def last_w(i):
        @pl.when(inner & (i + W_AHEAD < ROW_PARTS))
        def _():
            mate_w_to_peer(i + W_AHEAD)

        arrived(w_part(peer_out, c, g, i), wz["po"] + i)

        @pl.when(inner)
        def _():
            last_w_to_mate(i)

        last_w_to_y(i)

    depth = 2 * wrows

    def product(block, lanes):
        att_lanes = pl.ds(pl.multiple_of((block % 2) * depth, HEAD_DIM), depth)
        return jnp.dot(
            attf[block // 2, :, att_lanes], wf[block, :, lanes], preferred_element_type=jnp.float32
        )

    tiles = wide // tile
    early = ROW_PARTS - tiles

    @pl.loop(0, early)
    def _(i):
        last_w(i)

    arrived(w_piece(peer_in, c, 1 - g), wy["pi"])
    w_to_sub("pi", 1 - g, 1)
    each_part(lambda i: arrived(att_part(attf.at[1 - h], i), rx + i))
    arrived(w_shard(f, 1 - c), ws_own)
    for b in ("mate", "pi"):
        arrived(w_piece(wblock[b], 1 - c, g), ws[b])
        arrived(w_piece(wblock[b], 1 - c, 1 - g), ws[b] + 1)

    @pl.loop(0, tiles)
    def _(n):
        last_w(n + early)
        lanes = pl.ds(pl.multiple_of(n * tile, tile), tile)
        pacc[:, lanes] = product(f, lanes) + product(mate, lanes) + product(peer_in, lanes)

    w_to_sub("po", g, 0)

    @pl.loop(0, ROW_PARTS)
    def _(i):
        arrived(w_part(peer_out, c, 1 - g, i), wy["po"] + i)

    w_to_sub("po", 1 - g, 1)
    arrived(w_piece(peer_out, 1 - c, g), ws["po"])
    arrived(w_piece(peer_out, 1 - c, 1 - g), ws["po"] + 1)

    @pl.loop(0, tiles)
    def _(n):
        lanes = pl.ds(pl.multiple_of(n * tile, tile), tile)
        total = pacc[:, lanes] + product(peer_out, lanes)
        out[:, lanes] = (total * gate[:, lanes]).astype(jnp.bfloat16)

    def sent(src, name, offset=0):
        copy(src, src, sends(name) + offset, 0, sub_dev).wait_send()

    sent(w, "wown")
    for b in ("mate", "pi", "po"):
        for which in range(2):
            sent(w_piece(0, 0, 0), "wsub" + b + str(which))
    sent(w_piece(0, 0, 0), "wymate")
    sent(w_piece(0, 0, 0), "wypi")

    def common_sent(i):
        sent(att_part(aout, 0), "ax", i)

    each_part(common_sent)

    @pl.loop(0, ROW_PARTS)
    def _(i):
        sent(w_part(0, 0, 0, 0), "wypo", i)

    @pl.when(inner)
    def _():
        for n in "kv":
            for name in ("i_sub", "i_peer", "pi_sub"):
                sent(k, name + n)
        for name in ("w_in_out", "w_own_peer", "w_pi_out"):
            sent(w_piece(0, 0, 0), name)

        def inner_sent(i):
            sent(att_part(aout, 0), "aout", i)
            for name in ("o_peerk", "o_subk", "po_subk", "o_peerv", "o_subv", "po_subv"):
                sent(att_part(aout, 0), name, i)

        each_part(inner_sent)

        @pl.loop(0, ROW_PARTS)
        def _(i):
            for name in ("w_mate_peer", "wout"):
                sent(w_part(0, 0, 0, 0), name, i)

    assert sends.used <= send_sems.shape[0] and recvs.used <= recv_sems.shape[0]


def line_shards(
    queries, keys, values, out_weight, time_table, action_table, levels, actions, cycle_order
):
    rows, cols = queries.shape
    wrows, wide = out_weight.shape
    heads = cols // HEAD_DIM
    bf16, f32 = jnp.bfloat16, jnp.float32
    vmem, smem, anywhere = (
        pl.BlockSpec(memory_space=space) for space in (pltpu.VMEM, pltpu.SMEM, pl.ANY)
    )
    return pl.pallas_call(
        line_kernel,
        out_shape=jax.ShapeDtypeStruct((rows, wide), bf16),
        in_specs=[smem] * 3 + [anywhere] * 4 + [vmem] * 2,
        out_specs=vmem,
        scratch_shapes=[
            pltpu.VMEM((4, 2 * rows, cols), bf16),
            pltpu.VMEM((4, 2 * rows, cols), bf16),
            pltpu.VMEM((2, rows, cols), bf16),
            pltpu.VMEM((2 * heads, rows, HEAD_DIM), f32),
            pltpu.VMEM((2 * heads, rows, 2 * HEAD_DIM), f32),
            pltpu.VMEM((2, rows, cols), bf16),
            pltpu.VMEM((rows, cols), bf16),
            pltpu.VMEM((4, 2 * wrows, wide), bf16),
            pltpu.VMEM((rows, wide), f32),
            pltpu.VMEM((1, wide), f32),
            pltpu.SemaphoreType.DMA((120,)),
            pltpu.SemaphoreType.DMA((120,)),
            pltpu.SemaphoreType.DMA((4,)),
        ],
        compiler_params=pltpu.CompilerParams(
            collective_id=0, has_side_effects=True, vmem_limit_bytes=62 * 1024 * 1024
        ),
    )(
        cycle_order, levels, actions, queries, keys, values, out_weight, time_table, action_table
    )


def solution(mesh):
    in_specs = (
        P(("group", "frame", "sub"), "head"),
        P(("group", "frame", "sub"), "head"),
        P(("group", "frame", "sub"), "head"),
        P(("frame", "sub"), "head"),
        P(None, "head"),
        P(None, "head"),
        P("group"),
        P("group", None),
        P("group"),
    )
    out_specs = P(("group", "frame", "sub"), "head")
    in_line = all(mesh.shape[a] == n for a, n in (("group", 2), ("frame", 4), ("head", 2), ("sub", 2)))
    shards = line_shards if in_line else ring_shards
    return jax.shard_map(shards, mesh=mesh, in_specs=in_specs, out_specs=out_specs, check_vma=False)
```

```python
import functools

import jax
import jax.numpy as jnp
from jax import lax
from jax.experimental import pallas as pl
from jax.experimental.pallas import tpu as pltpu
from jax.sharding import PartitionSpec as P

HEAD_DIM = 128
LEVELS = 50
ACTIONS = 256
FWIN = 3
PIECES = 5
AHEAD = 2
ROW_PARTS = 10
W_AHEAD = 2 * AHEAD
GANG = 2
LOG2E = 1.4426950408889634
MESH = pl.DeviceIdType.MESH


def from_behind(array, axis, by):
    count = lax.axis_size(axis)
    return lax.ppermute(array, axis, [(i, (i + by) % count) for i in range(count)])


def attend_heads(query_rows, key_rows, value_rows, key_valid):
    query_count = query_rows.shape[0]
    length = key_rows.shape[0]
    row_width = query_rows.shape[1]
    head_count = row_width // HEAD_DIM
    query_heads = jnp.moveaxis(query_rows.reshape(query_count, head_count, HEAD_DIM), 1, 0)
    key_heads = jnp.moveaxis(key_rows.reshape(length, head_count, HEAD_DIM), 1, 0)
    value_heads = jnp.moveaxis(value_rows.reshape(length, head_count, HEAD_DIM), 1, 0)
    factor = HEAD_DIM ** (-0.5)

    def one_head(operands):
        query_one, key_one, value_one = operands
        scores = jnp.dot(query_one, key_one.T, preferred_element_type=jnp.float32) * factor
        scores = jnp.where(key_valid[None, :], scores, -1e30)
        largest = jnp.max(scores, axis=1, keepdims=True)
        weights = jnp.exp(scores - largest)
        totals = jnp.sum(weights, axis=1, keepdims=True)
        mixed_rows = jnp.dot(
            weights.astype(jnp.bfloat16), value_one, preferred_element_type=jnp.float32
        )
        return (mixed_rows / totals).astype(jnp.bfloat16)

    result = lax.map(one_head, (query_heads, key_heads, value_heads))
    return jnp.moveaxis(result, 0, 1).reshape(query_count, row_width)


def gate_of_slot(time_table, action_table, levels, actions):
    frame_slot = lax.axis_index("frame")
    level_onehot = (jnp.arange(LEVELS, dtype=jnp.int32) == levels[frame_slot]).astype(jnp.bfloat16)
    action_match = jnp.arange(ACTIONS, dtype=jnp.int32)[None, :] == actions[frame_slot][:, None]
    action_count = jnp.sum(action_match.astype(jnp.float32), axis=0).astype(jnp.bfloat16)
    gate_row = jnp.dot(level_onehot[None, :], time_table, preferred_element_type=jnp.float32)
    return gate_row + jnp.dot(
        action_count[None, :], action_table, preferred_element_type=jnp.float32
    )


def ring_shards(
    queries, keys, values, out_weight, time_table, action_table, levels, actions, cycle_order
):
    window = FWIN
    own_position = cycle_order[lax.axis_index("frame")]
    gate_row = gate_of_slot(time_table, action_table, levels, actions)
    paired = jnp.stack([keys, values])
    block_rows = paired.shape[1] * lax.axis_size("sub")
    local_pair = lax.all_gather(paired, "sub", axis=1, tiled=True)
    blocks = [local_pair]
    for distance in range(1, window):
        blocks.append(from_behind(local_pair, "frame", distance))
    joined = jnp.concatenate(blocks, axis=1)
    block_valid = own_position >= jnp.arange(window, dtype=jnp.int32)
    key_valid = jnp.repeat(block_valid, block_rows)
    attended = attend_heads(queries, joined[0], joined[1], key_valid)
    outputs = lax.all_gather(attended, "head", axis=1, tiled=True)
    all_rows = lax.all_gather(out_weight, ("frame", "sub"), axis=0, tiled=True)
    projected = jnp.dot(outputs, all_rows, preferred_element_type=jnp.float32)
    return (gate_row * projected).astype(jnp.bfloat16)


class Indices:
    def __init__(self, sems):
        self.sems, self.names, self.used = sems, {}, 0

    def __call__(self, name, count=1):
        if name not in self.names:
            self.names[name] = (self.used, count)
            self.used += count
        return self.names[name][0]


def line_kernel(
    cycle, levels, actions, q, k, v, w, time_table, action_rows_in, out,
    kb, vb, qb, stat, acc, attf, aout, wf, pacc, gate, action_table, send_sems, recv_sems, local_sems,
):
    rows, cols = q.shape
    wrows, wide = w.shape
    half = wrows // 2
    part = half // ROW_PARTS
    heads = cols // HEAD_DIM
    per = heads // PIECES
    att_cols = per * HEAD_DIM
    tile = 512
    keys_n = 2 * rows
    scale = HEAD_DIM ** (-0.5) * LOG2E

    g, f, h, c = (lax.axis_index(name) for name in ("group", "frame", "head", "sub"))
    side = f // 2
    f_in, f_out = 1 + side, 3 * side
    peer_in, peer_out = 2 - side, 3 - 3 * side
    inner = f == f_in
    mate = f_in + f_out - f
    sub_dev = (g, f, h, 1 - c)
    x_dev = (g, f, 1 - h, c)
    y_dev = (1 - g, f, h, c)
    mate_dev = (g, mate, h, c)
    peer_dev = (g, peer_in, h, c)

    barrier = pltpu.get_barrier_semaphore()
    for dev in (sub_dev, x_dev, y_dev, mate_dev):
        pl.semaphore_signal(barrier, inc=1, device_id=dev, device_id_type=MESH)

    @pl.when(inner)
    def _():
        pl.semaphore_signal(barrier, inc=1, device_id=peer_dev, device_id_type=MESH)
        pl.semaphore_wait(barrier, 5)

    @pl.when(jnp.logical_not(inner))
    def _():
        pl.semaphore_wait(barrier, 4)

    sends, recvs = Indices(send_sems), Indices(recv_sems)

    def copy(src, dst, send, recv, dev):
        return pltpu.make_async_remote_copy(
            src_ref=src,
            dst_ref=dst,
            send_sem=send_sems.at[send],
            recv_sem=recv_sems.at[recv],
            device_id=dev,
            device_id_type=MESH,
        )

    def arrived(dst, recv):
        copy(dst, dst, 0, recv, sub_dev).wait_recv()

    def own_rows(base, count, index):
        return pl.ds(pl.multiple_of(base + index * count, 16), count)

    def kv_half(buf, block, cc):
        return buf.at[block, own_rows(0, rows, cc), :]

    def kv_part(buf, block, cc, i):
        lanes = pl.ds(pl.multiple_of(i * att_cols, HEAD_DIM), att_cols)
        return buf.at[block, own_rows(0, rows, cc), lanes]

    def w_shard(block, cc):
        return wf.at[block, own_rows(0, wrows, cc), :]

    def w_piece(block, cc, gg):
        return wf.at[block, own_rows(cc * wrows, half, gg), :]

    def w_part(block, cc, gg, i):
        return wf.at[block, own_rows(cc * wrows + gg * half, part, i), :]

    def att_part(ref, i):
        return ref.at[:, pl.ds(pl.multiple_of(i * att_cols, HEAD_DIM), att_cols)]

    kv_z = lambda n, which: recvs("kvz" + n + which, 1 if which == "pi" else PIECES)
    kv_s = lambda n, which: recvs("kvs" + n + which, 1 if which in ("i", "pi") else PIECES)
    wz = {b: recvs("wz" + b, ROW_PARTS if b == "po" else 1) for b in ("mate", "pi", "po")}
    wy = {b: recvs("wy" + b, ROW_PARTS if b == "po" else 1) for b in ("mate", "pi", "po")}
    ws = {b: recvs("ws" + b, 4 if b == "po" else 2) for b in ("mate", "pi", "po")}
    ws_own, rq = recvs("wsown"), recvs("q")
    ra, rx = recvs("ra", PIECES), recvs("rx", PIECES)
    wblock = {"mate": mate, "pi": peer_in, "po": peer_out}

    def w_to_sub(b, gg, which):
        src = w_piece(wblock[b], c, gg)
        one = copy(src, src, sends("wsub" + b + str(which)), ws[b] + which, sub_dev)
        one.start()

    def last_w_to_sub(gg, which, i):
        src = wf.at[peer_out, own_rows(c * wrows + gg * half, half // 2, i), :]
        copy(src, src, sends("wlast" + str(which), 2) + i, ws["po"] + 2 * which + i, sub_dev).start()

    def last_w_from_sub(gg, which, i):
        dst = wf.at[peer_out, own_rows((1 - c) * wrows + gg * half, half // 2, i), :]
        arrived(dst, ws["po"] + 2 * which + i)

    def w_piece_to_y(b):
        src = w_piece(wblock[b], c, g)
        copy(src, src, sends("wy" + b), wy[b], y_dev).start()

    def last_w_to_y(i):
        src = w_part(peer_out, c, g, i)
        copy(src, src, sends("wypo", ROW_PARTS) + i, wy["po"] + i, y_dev).start()

    def last_w_to_mate(i):
        src = w_part(peer_out, c, g, i)
        copy(src, src, sends("wout", ROW_PARTS) + i, wz["po"] + i, mate_dev).start()

    def mate_w_to_peer(i):
        src = w_part(mate, c, g, i)
        copy(src, src, sends("w_mate_peer", ROW_PARTS) + i, wz["po"] + i, peer_dev).start()

    own_actions = pltpu.make_async_copy(action_rows_in, action_table, local_sems.at[4])

    def gate_rows():
        own_actions.wait()

        @pl.loop(0, wide // tile)
        def _(n):
            lanes = pl.ds(pl.multiple_of(n * tile, tile), tile)
            level_rows = time_table[:, lanes].astype(jnp.float32)
            level_at = lax.broadcasted_iota(jnp.int32, level_rows.shape, 0)
            total = jnp.sum(
                jnp.where(level_at == levels[f], level_rows, 0.0), axis=0, keepdims=True
            )
            action_rows = action_table[:, lanes].astype(jnp.float32)
            action_at = lax.broadcasted_iota(jnp.int32, action_rows.shape, 0)
            times = jnp.zeros(action_rows.shape, jnp.float32)
            for a in range(actions.shape[1]):
                times += (action_at == actions[f, a]).astype(jnp.float32)
            gate[:, lanes] = total + jnp.sum(times * action_rows, axis=0, keepdims=True)

    def valid_of(slot, block):
        distance = (slot - block + 4) % 4
        return cycle[block] == cycle[slot] - distance

    def attend(items):
        lanes = [
            pl.ds(pl.multiple_of(head * HEAD_DIM, HEAD_DIM), HEAD_DIM) for _, _, head, _ in items
        ]
        scores = [
            lax.dot_general(
                qb[si, :, at], kb[block, :, at], (((1,), (1,)), ((), ())),
                preferred_element_type=jnp.float32,
            )
            for (si, block, _, _), at in zip(items, lanes)
        ]
        ones = jnp.ones((keys_n, HEAD_DIM), jnp.bfloat16)
        results = []
        for (si, block, head, _), at, score in zip(items, lanes, scores):
            valid = valid_of(jnp.where(si == 0, f_in, f_out), block)
            old_max = stat[si * heads + head]
            block_max = jnp.where(valid, jnp.max(score, axis=1, keepdims=True), -1e30)
            new_max = jnp.maximum(old_max, block_max)
            base = jnp.where(valid, new_max, 1e30)
            weights = jnp.exp2((score - jnp.concatenate([base] * (keys_n // HEAD_DIM), 1)) * scale)
            fade = jnp.exp2((old_max - new_max) * scale)
            values = jnp.concatenate([vb[block, :, at], ones], 1)
            mixed = jnp.dot(
                weights.astype(jnp.bfloat16), values, preferred_element_type=jnp.float32
            )
            mixed += acc[si * heads + head] * jnp.concatenate([fade, fade], 1)
            results.append((new_max, mixed))
        for (si, _, head, finish), at, (new_max, mixed) in zip(items, lanes, results):
            if finish is None:
                acc[si * heads + head] = mixed
                stat[si * heads + head] = new_max
            else:
                rounded = (mixed[:, :HEAD_DIM] / mixed[:, HEAD_DIM:]).astype(jnp.bfloat16)
                finish[:, at] = rounded

    def units(si, block):
        @pl.loop(0, heads // GANG)
        def _(n):
            attend([(si, block, n * GANG + j, None) for j in range(GANG)])

    def each_part(body):
        @pl.loop(0, PIECES)
        def _(i):
            body(i)

    own_w = pltpu.make_async_copy(w, w_shard(f, c), local_sems.at[0])
    own_w.start()
    own_actions.start()
    w_to_partner = copy(w, w_shard(f, c), sends("wown"), ws_own, sub_dev)

    @pl.when(inner)
    def _():
        for n, ref, buf in (("k", k, kb), ("v", v, vb)):
            copy(ref, kv_half(buf, f, c), sends("i_sub" + n), kv_s(n, "i"), sub_dev).start()
            copy(ref, kv_half(buf, f, c), sends("i_peer" + n), kv_z(n, "pi"), peer_dev).start()
        locals_ = [
            pltpu.make_async_copy(k, kv_half(kb, f, c), local_sems.at[1]),
            pltpu.make_async_copy(v, kv_half(vb, f, c), local_sems.at[2]),
            pltpu.make_async_copy(q, qb.at[0], local_sems.at[3]),
        ]
        for one in locals_:
            one.start()
        w_to_partner.start()
        copy(
            w.at[own_rows(0, half, g), :], w_piece(f, c, g), sends("w_in_out"), wz["mate"], mate_dev
        ).start()

        @pl.loop(0, 2 * heads)
        def _(i):
            acc[i] = jnp.zeros((rows, 2 * HEAD_DIM), jnp.float32)
            stat[i] = jnp.full((rows, HEAD_DIM), -1e30, jnp.float32)

        gate_rows()

        for one in locals_:
            one.wait()
        for n, buf in (("k", kb), ("v", vb)):
            arrived(kv_half(buf, f, 1 - c), kv_s(n, "i"))
        units(0, f_in)
        own_w.wait()

        def relay(i):
            for n, buf in (("k", kb), ("v", vb)):
                src = kv_part(buf, f_out, c, i)
                arrived(src, kv_z(n, "o") + i)
                send = sends("o_peer" + n, PIECES) + i
                copy(src, src, send, kv_z(n, "po") + i, peer_dev).start()
                copy(src, src, sends("o_sub" + n, PIECES) + i, kv_s(n, "o") + i, sub_dev).start()

        src = w_piece(f, c, g)
        copy(src, src, sends("w_own_peer"), wz["pi"], peer_dev).start()
        for i in range(AHEAD):
            relay(i)
        for n, buf in (("k", kb), ("v", vb)):
            src = kv_half(buf, peer_in, c)
            arrived(src, kv_z(n, "pi"))
            copy(src, src, sends("pi_sub" + n), kv_s(n, "pi"), sub_dev).start()
        arrived(qb.at[1], rq)
        for n, buf in (("k", kb), ("v", vb)):
            arrived(kv_half(buf, peer_in, 1 - c), kv_s(n, "pi"))
        units(1, peer_in)
        arrived(w_piece(peer_in, c, g), wz["pi"])
        src = w_piece(peer_in, c, g)
        copy(src, src, sends("w_pi_out"), wz["pi"], mate_dev).start()
        w_piece_to_y("pi")
        w_to_sub("pi", g, 0)
        next_block = jnp.where(side == 0, f_out, peer_in)
        last_block = jnp.where(side == 0, peer_out, f_in)

        def last(i):
            @pl.when(i + AHEAD < PIECES)
            def _():
                relay(i + AHEAD)

            @pl.when(i == 1)
            def _():
                arrived(w_piece(mate, c, g), wz["mate"])
                w_piece_to_y("mate")
                w_to_sub("mate", g, 0)

            @pl.when(i + AHEAD >= PIECES)
            def _():
                for j in range(2):
                    mate_w_to_peer(2 * (i + AHEAD - PIECES) + j)

            for n, buf in (("k", kb), ("v", vb)):
                src = kv_part(buf, peer_out, c, i)
                arrived(src, kv_z(n, "po") + i)
                copy(src, src, sends("po_sub" + n, PIECES) + i, kv_s(n, "po") + i, sub_dev).start()
            for n, buf in (("k", kb), ("v", vb)):
                arrived(kv_part(buf, f_out, 1 - c, i), kv_s(n, "o") + i)

            @pl.loop(0, per)
            def _(j):
                head = i * per + j
                attend([(1, f_out, head, None), (0, next_block, head, None)])

            for n, buf in (("k", kb), ("v", vb)):
                arrived(kv_part(buf, peer_out, 1 - c, i), kv_s(n, "po") + i)

            @pl.loop(0, per)
            def _(j):
                head = i * per + j
                attend([(1, last_block, head, aout), (0, peer_out, head, attf.at[h])])

            src = att_part(aout, i)
            copy(src, att_part(attf.at[h], i), sends("aout", PIECES) + i, ra + i, mate_dev).start()
            src = att_part(attf.at[h], i)
            copy(src, src, sends("ax", PIECES) + i, rx + i, x_dev).start()

        each_part(last)
        arrived(w_piece(mate, c, 1 - g), wy["mate"])
        w_to_sub("mate", 1 - g, 1)

    @pl.when(jnp.logical_not(inner))
    def _():
        def kv_out(i):
            lanes = pl.ds(pl.multiple_of(i * att_cols, HEAD_DIM), att_cols)
            return [
                copy(
                    ref.at[:, lanes], kv_part(buf, f, c, i), sends("out_" + n, PIECES) + i,
                    kv_z(n, "o") + i, mate_dev,
                )
                for n, ref, buf in (("k", k, kb), ("v", v, vb))
            ]

        def kv_start(i):
            for one in kv_out(i):
                one.start()

        def kv_sent(i):
            for one in kv_out(i):
                one.wait_send()

        q_copy = copy(q, qb.at[1], sends("out_q"), rq, mate_dev)
        q_copy.start()
        kv_start(0)
        w_to_partner.start()
        own_w.wait()
        arrived(w_piece(mate, c, g), wz["mate"])
        w_piece_to_y("mate")
        w_to_sub("mate", g, 0)
        q_copy.wait_send()

        src = w_piece(f, c, g)
        w_copy = copy(src, src, sends("out_w"), wz["mate"], mate_dev)

        @pl.loop(1, PIECES)
        def _(i):
            @pl.when(i == 3)
            def _():
                w_copy.start()

            kv_start(i)
            kv_sent(i - 1)

        kv_sent(PIECES - 1)
        gate_rows()
        arrived(w_piece(mate, c, 1 - g), wy["mate"])
        w_to_sub("mate", 1 - g, 1)
        arrived(w_piece(peer_in, c, g), wz["pi"])
        w_piece_to_y("pi")
        w_to_sub("pi", g, 0)
        w_copy.wait_send()

        def back(i):
            src = att_part(attf.at[h], i)
            arrived(src, ra + i)
            copy(src, src, sends("ax", PIECES) + i, rx + i, x_dev).start()

        each_part(back)

    def last_w(i):
        @pl.when(inner & (i + W_AHEAD < ROW_PARTS))
        def _():
            mate_w_to_peer(i + W_AHEAD)

        arrived(w_part(peer_out, c, g, i), wz["po"] + i)

        @pl.when(inner)
        def _():
            last_w_to_mate(i)

        last_w_to_y(i)

    depth = 2 * wrows

    def product(block, lanes):
        att_lanes = pl.ds(pl.multiple_of((block % 2) * depth, HEAD_DIM), depth)
        return jnp.dot(
            attf[block // 2, :, att_lanes], wf[block, :, lanes], preferred_element_type=jnp.float32
        )

    tiles = wide // tile
    early = ROW_PARTS - tiles

    @pl.loop(0, early)
    def _(i):
        last_w(i)

    last_w_to_sub(g, 0, 0)
    arrived(w_piece(peer_in, c, 1 - g), wy["pi"])
    w_to_sub("pi", 1 - g, 1)
    each_part(lambda i: arrived(att_part(attf.at[1 - h], i), rx + i))
    arrived(w_shard(f, 1 - c), ws_own)
    for b in ("mate", "pi"):
        arrived(w_piece(wblock[b], 1 - c, g), ws[b])
        arrived(w_piece(wblock[b], 1 - c, 1 - g), ws[b] + 1)

    @pl.loop(0, tiles)
    def _(n):
        last_w(n + early)
        lanes = pl.ds(pl.multiple_of(n * tile, tile), tile)
        pacc[:, lanes] = product(f, lanes) + product(mate, lanes) + product(peer_in, lanes)

    last_w_to_sub(g, 0, 1)
    for i in range(2):

        @pl.loop(i * (ROW_PARTS // 2), (i + 1) * (ROW_PARTS // 2))
        def _(j):
            arrived(w_part(peer_out, c, 1 - g, j), wy["po"] + j)

        last_w_to_sub(1 - g, 1, i)
    for which, gg in ((0, g), (1, 1 - g)):
        for i in range(2):
            last_w_from_sub(gg, which, i)

    @pl.loop(0, tiles)
    def _(n):
        lanes = pl.ds(pl.multiple_of(n * tile, tile), tile)
        total = pacc[:, lanes] + product(peer_out, lanes)
        out[:, lanes] = (total * gate[:, lanes]).astype(jnp.bfloat16)

    def sent(src, name, offset=0):
        copy(src, src, sends(name) + offset, 0, sub_dev).wait_send()

    sent(w, "wown")
    for b in ("mate", "pi"):
        for which in range(2):
            sent(w_piece(0, 0, 0), "wsub" + b + str(which))
    for which in range(2):
        for i in range(2):
            sent(wf.at[0, own_rows(0, half // 2, 0), :], "wlast" + str(which), i)
    sent(w_piece(0, 0, 0), "wymate")
    sent(w_piece(0, 0, 0), "wypi")

    def common_sent(i):
        sent(att_part(aout, 0), "ax", i)

    each_part(common_sent)

    @pl.loop(0, ROW_PARTS)
    def _(i):
        sent(w_part(0, 0, 0, 0), "wypo", i)

    @pl.when(inner)
    def _():
        for n in "kv":
            for name in ("i_sub", "i_peer", "pi_sub"):
                sent(k, name + n)
        for name in ("w_in_out", "w_own_peer", "w_pi_out"):
            sent(w_piece(0, 0, 0), name)

        def inner_sent(i):
            sent(att_part(aout, 0), "aout", i)
            for name in ("o_peerk", "o_subk", "po_subk", "o_peerv", "o_subv", "po_subv"):
                sent(att_part(aout, 0), name, i)

        each_part(inner_sent)

        @pl.loop(0, ROW_PARTS)
        def _(i):
            for name in ("w_mate_peer", "wout"):
                sent(w_part(0, 0, 0, 0), name, i)

    assert sends.used <= send_sems.shape[0] and recvs.used <= recv_sems.shape[0]


def line_shards(
    queries, keys, values, out_weight, time_table, action_table, levels, actions, cycle_order
):
    rows, cols = queries.shape
    wrows, wide = out_weight.shape
    heads = cols // HEAD_DIM
    bf16, f32 = jnp.bfloat16, jnp.float32
    vmem, smem, anywhere = (
        pl.BlockSpec(memory_space=space) for space in (pltpu.VMEM, pltpu.SMEM, pl.ANY)
    )
    return pl.pallas_call(
        line_kernel,
        out_shape=jax.ShapeDtypeStruct((rows, wide), bf16),
        in_specs=[smem] * 3 + [anywhere] * 4 + [vmem, anywhere],
        out_specs=vmem,
        scratch_shapes=[
            pltpu.VMEM((4, 2 * rows, cols), bf16),
            pltpu.VMEM((4, 2 * rows, cols), bf16),
            pltpu.VMEM((2, rows, cols), bf16),
            pltpu.VMEM((2 * heads, rows, HEAD_DIM), f32),
            pltpu.VMEM((2 * heads, rows, 2 * HEAD_DIM), f32),
            pltpu.VMEM((2, rows, cols), bf16),
            pltpu.VMEM((rows, cols), bf16),
            pltpu.VMEM((4, 2 * wrows, wide), bf16),
            pltpu.VMEM((rows, wide), f32),
            pltpu.VMEM((1, wide), f32),
            pltpu.VMEM(action_table.shape, bf16),
            pltpu.SemaphoreType.DMA((120,)),
            pltpu.SemaphoreType.DMA((120,)),
            pltpu.SemaphoreType.DMA((5,)),
        ],
        compiler_params=pltpu.CompilerParams(
            collective_id=0, has_side_effects=True, vmem_limit_bytes=62 * 1024 * 1024
        ),
    )(
        cycle_order, levels, actions, queries, keys, values, out_weight, time_table, action_table
    )


def solution(mesh):
    in_specs = (
        P(("group", "frame", "sub"), "head"),
        P(("group", "frame", "sub"), "head"),
        P(("group", "frame", "sub"), "head"),
        P(("frame", "sub"), "head"),
        P(None, "head"),
        P(None, "head"),
        P("group"),
        P("group", None),
        P("group"),
    )
    out_specs = P(("group", "frame", "sub"), "head")
    in_line = all(mesh.shape[a] == n for a, n in (("group", 2), ("frame", 4), ("head", 2), ("sub", 2)))
    shards = line_shards if in_line else ring_shards
    return jax.shard_map(shards, mesh=mesh, in_specs=in_specs, out_specs=out_specs, check_vma=False)
```
